128 devices in a mesh: seq: 32 (over z, x, core), batch: 4 (over y).
Axes of the slice: x: 4, y: 4, z: 4, core: 2. Of those that a mesh axis runs over, the one named last changes fastest.
Arguments:
- query_rows: bfloat16 [4, 4096, 1024], P('batch', 'seq'), may hold values from -6 to 6
- key_rows: bfloat16 [4, 4096, 1024], P('batch', 'seq'), may hold values from -6 to 6
- value_rows: bfloat16 [4, 4096, 2048], P('batch', 'seq'), may hold values from -6 to 6
- gate_z: bfloat16 [4, 4096, 2048], P('batch', 'seq'), may hold values from -6 to 6
- log_decay: float32 [4, 16, 4096], P('batch', None, 'seq'), may hold values from -0.7 to 0
- write_strength: float32 [4, 16, 4096], P('batch', None, 'seq'), may hold values from 0.0005 to 0.1
- norm_gain: float32 [128], replicated, may hold values from 0.1 to 1.9
- out_weight: bfloat16 [2048, 2048], replicated, may hold values from -0.125 to 0.125
- residual: bfloat16 [4, 4096, 2048], P('batch', 'seq'), may hold values from -6 to 6
- post_gain: float32 [2048], replicated, may hold values from 0.1 to 1.9
- expert_ids: int32 [4, 4096, 10], P('batch', 'seq'), may hold values from 0 to 255, all different within a row; in each aligned block of 128 rows (0 to 127, 128 to 255, ..., all dimensions but the last counted through in order) at most 7 rows name the same one
- gate_scores: float32 [4, 4096, 10], P('batch', 'seq'), may hold values from 0.1 to 1
- expert_up: bfloat16 [256, 2048, 1024], P(('seq', 'batch')), may hold values from -0.125 to 0.125
- expert_down: bfloat16 [256, 512, 2048], P(('seq', 'batch')), may hold values from -0.25 to 0.25
Outputs:
- mixed: bfloat16 [4, 4096, 2048], P('batch', 'seq')
The draws below stay inside these ranges and needn't reach their ends.
Inputs may be any that keep to these rules, and one draw needn't show every extreme that they name: `expert_ids`: each row names 10 different experts; among the rows of one device no expert is named by more than 7 rows, a bound that some block reaches.
All inputs are finite; a program needn't handle non-finite values.
Results may differ from the reference program's by a relative error of at most 0.005.
Values may be sent and summed in bfloat16 or wider, within the bound.
A program may use at most 256 MiB of HBM per device.

```python
import math
import jax
import jax.numpy as jnp
import numpy as np
from jax import lax

D = 2048
HV = 16
HK = 8
DK = 128
DV = 128
FFE = 512
TOP = 10
SPAN = 64
TOK_DEV = 128
PROMPTS = 4
QUERY_SPAN_SIZE = 4096
EXPERTS = 256
CAP = 7
N_SEQ = 32


def draw_log_decay(key, part):
    key = jax.random.fold_in(key, 7)
    derived_seed_list = jax.random.split(key, 7)
    entire_dimensions = (PROMPTS, HV, QUERY_SPAN_SIZE)
    fast_share = 0.5
    fast = jax.random.uniform(derived_seed_list[0], (PROMPTS, HV, 1)) < fast_share
    fast_rate = jnp.exp(jax.random.uniform(derived_seed_list[1], (PROMPTS, HV, 1), minval=math.log(1.0 / 50.0), maxval=math.log(1.0 / 30.0)))
    slow_rate = jnp.exp(jax.random.uniform(derived_seed_list[2], (PROMPTS, HV, 1), minval=math.log(0.02 / QUERY_SPAN_SIZE), maxval=math.log(0.3 / QUERY_SPAN_SIZE)))
    forgetting_speed = jnp.where(fast, fast_rate, slow_rate)
    blocks = QUERY_SPAN_SIZE // TOK_DEV
    multiplier_coefficient = jnp.exp(jax.random.uniform(derived_seed_list[3], (PROMPTS, HV, blocks, 1), minval=math.log(0.5), maxval=math.log(2.0)))
    multiplier_coefficient = jnp.broadcast_to(multiplier_coefficient, (PROMPTS, HV, blocks, TOK_DEV)).reshape(entire_dimensions)
    approximate_guess = jax.random.uniform(derived_seed_list[4], entire_dimensions, minval=0.5, maxval=1.5)
    contiguous_span = jax.random.uniform(derived_seed_list[5], entire_dimensions) < 3.0 / QUERY_SPAN_SIZE
    discarded_positions = jnp.log(jax.random.uniform(derived_seed_list[6], entire_dimensions, minval=0.6, maxval=0.85))
    return (-(forgetting_speed * multiplier_coefficient * approximate_guess) + jnp.where(contiguous_span, discarded_positions, 0.0)).astype(jnp.float32)


def shard_levels(key, extent, cuts, least, top_value):
    def one(dim, blocks):
        steps = jax.random.uniform(jax.random.fold_in(jax.random.fold_in(key, 6), dim), (blocks,), jnp.float32, least / len(cuts), top_value / len(cuts))
        return jnp.repeat(jnp.exp(steps), extent[dim] // blocks).reshape((-1,) + (1,) * (len(extent) - dim - 1))

    factor_of = one(*cuts[0])
    for cut in cuts[1:]:
        factor_of = factor_of * one(*cut)
    return factor_of


def routed_block(own_key, own, number, rows, number_of, top, most, skew):
    order = jax.random.permutation(own_key, number_of)
    crowded, usual = shares(number_of, rows * top, most, skew, True), shares(number_of, rows * top, most, skew, False)
    places = jnp.arange(number_of)

    def named(tallies, offset_by):
        used = int((tallies > 0).sum())
        fixed = max(1, used // 4)
        shifted = fixed + (places - fixed + offset_by * (used - fixed)) % max(1, number_of - fixed)
        return jnp.zeros((number_of,), jnp.int32).at[order[jnp.where(places < fixed, places, shifted)]].set(jnp.asarray(tallies, jnp.int32))

    tallies = jnp.where(number % 4 == 0, named(crowded, number // 4), named(usual, number - number // 4 - 1))
    mixed = jax.random.permutation(jax.random.fold_in(own, 3), number_of)
    source_of, taker = mixed[0:number_of // 2 * 2:2], mixed[1:number_of // 2 * 2:2]
    margin = jnp.minimum(tallies[source_of] - 1, most - tallies[taker]) // 2
    margin = jnp.where((source_of == order[0]) | (taker == order[0]) | (tallies[taker] == 0), 0, jnp.maximum(margin, 0))
    shifted = jax.random.randint(jax.random.fold_in(own, 4), (number_of // 2,), 0, 1 << 20) % (margin + 1)
    tallies = tallies.at[source_of].add(-shifted).at[taker].add(shifted)
    items = jnp.searchsorted(jnp.cumsum(tallies), jnp.arange(rows * top), side="right").astype(jnp.int32)
    listing = items.reshape(top, rows).T
    listing = listing[jax.random.permutation(jax.random.fold_in(own, 1), rows)]
    offset_by = jax.random.randint(jax.random.fold_in(own, 2), (rows, 1), 0, top)
    return jnp.take_along_axis(listing, (jnp.arange(top)[None, :] + offset_by) % top, axis=1)


def shares(number_of, total, reach, lean, full):
    portions = [(1 << 20) // math.isqrt(grade ** lean) + 1 for grade in range(1, number_of + 1)]
    largest = reach if full else min(reach, max(-(-total // number_of), total * portions[0] // sum(portions)))
    least = 1 if total - largest >= number_of - 1 else 0
    given, spare = [largest] + [least] * (number_of - 1), total - largest - least * (number_of - 1)
    while spare > 0:
        free = [i for i in range(1, number_of) if given[i] < largest] or [i for i in range(1, number_of) if given[i] < reach]
        mass, remaining = sum([portions[i] for i in free]), spare
        for i in free:
            addition = min(reach - given[i], max(1, remaining * portions[i] // mass), spare)
            given[i] = given[i] + addition
            spare = spare - addition
    return np.array(given)


def normal_values(rng, extent, scale, limit, cuts=(), held_as=jnp.bfloat16):
    values = jax.random.normal(rng, extent, jnp.float32) * scale
    if len(cuts) > 0:
        values = shard_levels(rng, extent, cuts, -0.22, 0.18) * values
    return jnp.clip(values, min=-limit, max=limit).astype(held_as)


def setup_inputs(seed: int = 0) -> dict:
    streams_of = jax.random.split(jax.random.key(seed), 15)
    query_rows = normal_values(streams_of[0], (PROMPTS, QUERY_SPAN_SIZE, HK * DK), 1.0, 6.0, ((0, 4), (1, 32)))
    key_rows = normal_values(streams_of[1], (PROMPTS, QUERY_SPAN_SIZE, HK * DK), 1.0, 6.0, ((0, 4), (1, 32)))
    value_rows = normal_values(streams_of[2], (PROMPTS, QUERY_SPAN_SIZE, HV * DV), 1.0, 6.0, ((0, 4), (1, 32)))
    gate_z = normal_values(streams_of[3], (PROMPTS, QUERY_SPAN_SIZE, HV * DV), 1.0, 6.0, ((0, 4), (1, 32)))
    log_decay = draw_log_decay(jax.random.fold_in(streams_of[14], 71), 0)
    write_strength = jnp.clip(jnp.exp(math.log(0.1) - 5.2983173 * jax.random.uniform(streams_of[5], (PROMPTS, HV, QUERY_SPAN_SIZE), jnp.float32) ** shard_levels(streams_of[5], (PROMPTS, HV, QUERY_SPAN_SIZE), ((0, 4), (2, 32)), -0.2, 0.2)), 0.0005, 0.1)
    norm_gain = jnp.clip(1.0 + 0.18 * jax.random.normal(streams_of[6], (DV,), jnp.float32), 0.1, 1.9)
    out_weight = normal_values(streams_of[7], (HV * DV, D), (HV * DV) ** -0.5, 0.125)
    residual = normal_values(streams_of[8], (PROMPTS, QUERY_SPAN_SIZE, D), 1.0, 6.0, ((0, 4), (1, 32)))
    post_gain = jnp.clip(1.0 + 0.18 * jax.random.normal(streams_of[9], (D,), jnp.float32), 0.1, 1.9)
    expert_ids_keys = jax.random.split(jax.random.fold_in(streams_of[10], 1), PROMPTS * QUERY_SPAN_SIZE // TOK_DEV)
    expert_ids_turns = jax.random.permutation(jax.random.fold_in(streams_of[10], 3), PROMPTS * QUERY_SPAN_SIZE // TOK_DEV)
    expert_ids = jax.vmap(lambda own, number: routed_block(jax.random.fold_in(streams_of[10], 2), own, number, TOK_DEV, EXPERTS, TOP, CAP, 2))(expert_ids_keys, expert_ids_turns).reshape((PROMPTS, QUERY_SPAN_SIZE, TOP))
    gate_scores = jnp.clip(jnp.exp(math.log(1.0) - 2.3025851 * jax.random.uniform(streams_of[11], (PROMPTS, QUERY_SPAN_SIZE, TOP), jnp.float32) ** shard_levels(streams_of[11], (PROMPTS, QUERY_SPAN_SIZE, TOP), ((0, 4), (1, 32)), -0.2, 0.2)), 0.1, 1.0)
    expert_up = normal_values(streams_of[12], (EXPERTS, D, 2 * FFE), D ** -0.5, 0.125, ((0, 128),))
    expert_down = normal_values(streams_of[13], (EXPERTS, FFE, D), FFE ** -0.5, 0.25, ((0, 128),))
    return dict(query_rows=query_rows, key_rows=key_rows, value_rows=value_rows, gate_z=gate_z, log_decay=log_decay, write_strength=write_strength, norm_gain=norm_gain, out_weight=out_weight, residual=residual, post_gain=post_gain, expert_ids=expert_ids, gate_scores=gate_scores, expert_up=expert_up, expert_down=expert_down)


PRECISE = lax.Precision.HIGHEST
EPSILON = 1e-06

def unit_rows(tensor):
    return tensor / jnp.sqrt(lax.optimization_barrier(jnp.sum(tensor * tensor, axis=-1, keepdims=True)) + EPSILON)

def block_terms(query_in, key_in, value_in, decay_in, strength_in, block, head_dim):
    head_count, length = decay_in.shape
    nblocks = length // block
    query_unit = unit_rows(query_in.astype(jnp.float32).reshape(length, -1, head_dim)) * head_dim ** (-0.5)
    key_unit = unit_rows(key_in.astype(jnp.float32).reshape(length, -1, head_dim))
    group_size = head_count // query_unit.shape[1]
    value_full = value_in.astype(jnp.float32).reshape(length, head_count, -1)
    value_width = value_full.shape[-1]

    def split_heads(tensor):
        return jnp.transpose(tensor, (1, 0, 2)).reshape(head_count, nblocks, block, tensor.shape[-1])
    query_blk = split_heads(jnp.repeat(query_unit, group_size, axis=1))
    key_blk = split_heads(jnp.repeat(key_unit, group_size, axis=1))
    value_blk = split_heads(value_full)
    cum_decay = jnp.cumsum(decay_in.reshape(head_count, nblocks, block), axis=-1)
    beta_block = strength_in.reshape(head_count, nblocks, block)
    decay_gap = cum_decay[..., :, None] - cum_decay[..., None, :]
    strict = jnp.tril(jnp.ones((block, block), dtype=bool), -1)
    inclusive = jnp.tril(jnp.ones((block, block), dtype=bool), 0)
    decay_strict = jnp.where(strict, jnp.exp(jnp.where(strict, decay_gap, 0.0)), 0.0)
    decay_incl = jnp.where(inclusive, jnp.exp(jnp.where(inclusive, decay_gap, 0.0)), 0.0)
    key_key = jnp.einsum('hncd,hnjd->hncj', key_blk, key_blk, precision=PRECISE)
    query_key = jnp.einsum('hncd,hnjd->hncj', query_blk, key_blk, precision=PRECISE)
    gamma = jnp.exp(cum_decay)
    system = jnp.eye(block, dtype=jnp.float32) + beta_block[..., None] * decay_strict * key_key
    rhs = jnp.concatenate([beta_block[..., None] * value_blk, (beta_block * gamma)[..., None] * key_blk], axis=-1)
    solved = lax.linalg.triangular_solve(system, rhs, left_side=True, lower=True, unit_diagonal=True)
    write_v = solved[..., :value_width]
    write_k = solved[..., value_width:]
    tail_keys = jnp.exp(cum_decay[..., -1:] - cum_decay)[..., None] * key_blk
    ident = jnp.eye(head_dim, dtype=jnp.float32)
    trans = gamma[..., -1][..., None, None] * ident - jnp.einsum('hncd,hnce->hnde', tail_keys, write_k, precision=PRECISE)
    inject = jnp.einsum('hncd,hnce->hnde', tail_keys, write_v, precision=PRECISE)
    scores = decay_incl * query_key
    reader = gamma[..., None] * query_blk - jnp.einsum('hncj,hnjd->hncd', scores, write_k, precision=PRECISE)
    local = jnp.einsum('hncj,hnje->hnce', scores, write_v, precision=PRECISE)
    return (trans, inject, reader, local)

def gated_norm(retained, gate_in, norm_gain):
    length, head_count, value_width = retained.shape
    gate_full = gate_in.astype(jnp.float32).reshape(length, head_count, value_width)
    scaled = retained * lax.rsqrt(lax.optimization_barrier(jnp.mean(retained * retained, axis=-1, keepdims=True)) + EPSILON)
    normed = scaled * norm_gain * jax.nn.silu(gate_full)
    return normed.astype(jnp.bfloat16).reshape(length, head_count * value_width)

def reference(query_rows, key_rows, value_rows, gate_z, log_decay, write_strength, norm_gain, out_weight, residual, post_gain, expert_ids, gate_scores, expert_up, expert_down):

    def one_prompt(pieces):
        query_in, key_in, value_in, gate_in, decay_in, strength_in, resid_in = pieces
        trans, inject, reader, local = block_terms(query_in, key_in, value_in, decay_in, strength_in, SPAN, DK)
        head_count = trans.shape[0]

        def advance(carried, block_items):
            step_trans, step_inject, step_reader, step_local = block_items
            emitted = jnp.einsum('hcd,hde->hce', step_reader, carried, precision=PRECISE) + step_local
            carried = jnp.einsum('hde,hef->hdf', step_trans, carried, precision=PRECISE) + step_inject
            return (carried, emitted)
        block_items = tuple((jnp.moveaxis(tensor, 1, 0) for tensor in (trans, inject, reader, local)))
        _, emitted = lax.scan(advance, jnp.zeros((head_count, DK, DV), jnp.float32), block_items)
        retained = jnp.transpose(emitted, (1, 0, 2, 3)).reshape(head_count, -1, DV).transpose(1, 0, 2)
        normed = gated_norm(retained, gate_in, norm_gain)
        mid = resid_in.astype(jnp.float32) + jnp.dot(normed.astype(jnp.float32), out_weight.astype(jnp.float32), preferred_element_type=jnp.float32)
        moe_in = (mid * lax.rsqrt(lax.optimization_barrier(jnp.mean(mid * mid, axis=-1, keepdims=True)) + EPSILON) * post_gain).astype(jnp.bfloat16)
        return (mid, moe_in)
    mid, moe_in = lax.map(one_prompt, (query_rows, key_rows, value_rows, gate_z, log_decay, write_strength, residual))
    model_width = mid.shape[-1]
    flat_in = moe_in.reshape(-1, model_width)
    token_total = flat_in.shape[0]
    flat_ids = expert_ids.reshape(-1).astype(jnp.int32)
    weights = (gate_scores / lax.optimization_barrier(jnp.sum(gate_scores, axis=-1, keepdims=True))).reshape(-1)
    order = jnp.argsort(flat_ids, stable=True).astype(jnp.int32)
    counts = jnp.bincount(flat_ids, length=EXPERTS).astype(jnp.int32)
    starts = (jnp.cumsum(counts) - counts).astype(jnp.int32)
    bound = PROMPTS * N_SEQ * CAP
    order_pad = jnp.concatenate([order, jnp.zeros((bound,), jnp.int32)])

    def one_expert(total, expert):
        picks = lax.dynamic_slice(order_pad, (starts[expert].astype(jnp.int32),), (bound,))
        valid = jnp.arange(bound, dtype=jnp.int32) < counts[expert]
        tokens = (picks // TOP).astype(jnp.int32)
        rows = flat_in[tokens]
        both = jnp.dot(rows.astype(jnp.float32), expert_up[expert].astype(jnp.float32), preferred_element_type=jnp.float32)
        hidden = (jax.nn.silu(both[:, :FFE]) * both[:, FFE:]).astype(jnp.bfloat16)
        result = jnp.dot(hidden.astype(jnp.float32), expert_down[expert].astype(jnp.float32), preferred_element_type=jnp.float32).astype(jnp.bfloat16)
        term = jnp.where(valid[:, None], weights[picks][:, None] * result.astype(jnp.float32), 0.0)
        return (total.at[tokens].add(term), None)
    total, _ = lax.scan(one_expert, jnp.zeros((token_total, model_width), jnp.float32), jnp.arange(EXPERTS, dtype=jnp.int32))
    mixed = mid.reshape(-1, model_width) + total
    return mixed.astype(jnp.bfloat16).reshape(mid.shape)
```

```python
import jax
import jax.numpy as jnp
from jax import lax
from jax.experimental import pallas as pl
from jax.experimental.pallas import tpu as pltpu
from jax.sharding import PartitionSpec as P

TOK = 128
DK = 128
HV = 16
HK = 8
GROUPS = 2
ROWS = 8
MSG = 208
EPSILON = 1e-06
PRECISE = lax.Precision.HIGHEST
F32 = jnp.float32
BF16 = jnp.bfloat16

NN = (((1,), (0,)), ((), ()))
NT = (((1,), (1,)), ((), ()))
TN = (((0,), (0,)), ((), ()))


def mul(a, b, dims=NN):
    return lax.dot_general(a, b, dims, preferred_element_type=F32)


def mul_precise(a, b, dims=NN):
    return lax.dot_general(a, b, dims, preferred_element_type=F32, precision=PRECISE)


def halves(a):
    high = a.astype(BF16)
    return high, (a - high.astype(F32)).astype(BF16)


def local_kernel(q_ref, k_ref, v_ref, ld_ref, bt_ref, msg_ref, reader_ref, local_ref, n_ref, x_ref, s_ref):
    heads = HV // GROUPS
    row = lax.broadcasted_iota(jnp.int32, (TOK, TOK), 0)
    col = lax.broadcasted_iota(jnp.int32, (TOK, TOK), 1)
    ld = ld_ref[0]
    cum_row = mul_precise(ld, (row <= col).astype(F32))
    cum_col = mul_precise((row >= col).astype(F32), ld, NT)
    beta_col = bt_ref[0].T
    units = []
    for g in range(heads // 2):
        lanes = slice(g * DK, (g + 1) * DK)
        k_raw = k_ref[:, lanes]
        q_raw = q_ref[:, lanes]
        k_full = k_raw.astype(F32)
        q_full = q_raw.astype(F32)
        k_scale = lax.rsqrt(jnp.sum(k_full * k_full, axis=-1, keepdims=True) + EPSILON)
        q_scale = lax.rsqrt(jnp.sum(q_full * q_full, axis=-1, keepdims=True) + EPSILON) * DK ** (-0.5)
        k_unit = k_full * k_scale
        k_high, k_low = halves(k_unit)
        right = jnp.concatenate([k_high, k_low], axis=1)
        key_key = mul(jnp.concatenate([k_raw, k_raw], axis=1), right, NT) * k_scale
        query_key = mul(jnp.concatenate([q_raw, q_raw], axis=1), right, NT) * q_scale
        units.append((k_unit, q_full * q_scale))
        for h in (2 * g, 2 * g + 1):
            gap = cum_col[:, h:h + 1] - cum_row[h:h + 1, :]
            decay = jnp.where(row >= col, jnp.exp(jnp.minimum(gap, 0.0)), 0.0)
            s_ref[h] = (decay * query_key).astype(BF16)
            system = jnp.where(row > col, decay * key_key, 0.0) * beta_col[:, h:h + 1]
            n_ref[h] = system
            x_ref[h] = jnp.where((row ^ col) == 1, -system, 0.0)
    for level in range(1, 7):
        cross = ((row >> level) ^ (col >> level)) == 1
        left = []
        for h in range(heads):
            part = jnp.where(cross, n_ref[h], 0.0)
            left.append(part + mul(x_ref[h].astype(BF16), part.astype(BF16)))
        for h in range(heads):
            old = x_ref[h]
            x_ref[h] = old - left[h] - mul(left[h].astype(BF16), old.astype(BF16))
    for h in range(heads):
        k_unit, q_unit = units[h // 2]
        cum = cum_col[:, h:h + 1]
        last = cum_row[h:h + 1, TOK - 1:TOK]
        beta = beta_col[:, h:h + 1]
        gamma = jnp.exp(cum)
        value = v_ref[:, h * DK:(h + 1) * DK].astype(F32) * beta
        right = jnp.concatenate([value, k_unit * (beta * gamma)], axis=1)
        write = (right + mul(x_ref[h].astype(BF16), right.astype(BF16))).astype(BF16)
        tail = (jnp.exp(last - cum) * k_unit).astype(BF16)
        moved = mul(write, tail, TN)
        trans = (-moved[DK:]).astype(BF16)
        inject = moved[:DK].astype(BF16)
        read = mul(s_ref[h], write)
        local_ref[h] = read[:, :DK]
        reader_ref[h] = (gamma * q_unit - read[:, DK:]).astype(BF16)
        whole = jnp.exp(jnp.broadcast_to(last, (16, DK)))
        part0 = whole.astype(BF16)
        part1 = (whole - part0.astype(F32)).astype(BF16)
        part2 = (whole - part0.astype(F32) - part1.astype(F32)).astype(BF16)
        line = lax.broadcasted_iota(jnp.int32, (16, DK), 0)
        parts = jnp.where(line == 0, part0.astype(F32), jnp.where(line == 1, part1.astype(F32), part2.astype(F32)))
        parts = jnp.where(line < 3, parts, 0.0).astype(BF16)
        for half in range(2):
            msg_ref[2 * h + half, 0:128] = trans
            msg_ref[2 * h + half, 128:192] = inject[half * 64:(half + 1) * 64]
            msg_ref[2 * h + half, 192:208] = parts


def local_terms(query, key, value, log_decay, strength):
    heads = HV // GROUPS
    return pl.pallas_call(
        local_kernel,
        grid=(GROUPS,),
        in_specs=[
            pl.BlockSpec((TOK, heads // 2 * DK), lambda i: (0, i)),
            pl.BlockSpec((TOK, heads // 2 * DK), lambda i: (0, i)),
            pl.BlockSpec((TOK, heads * DK), lambda i: (0, i)),
            pl.BlockSpec((1, heads, TOK), lambda i: (i, 0, 0)),
            pl.BlockSpec((1, heads, TOK), lambda i: (i, 0, 0)),
        ],
        out_specs=[
            pl.BlockSpec((2 * heads, MSG, DK), lambda i: (i, 0, 0)),
            pl.BlockSpec((heads, TOK, DK), lambda i: (i, 0, 0)),
            pl.BlockSpec((heads, TOK, DK), lambda i: (i, 0, 0)),
        ],
        out_shape=[
            jax.ShapeDtypeStruct((2 * HV, MSG, DK), BF16),
            jax.ShapeDtypeStruct((HV, TOK, DK), BF16),
            jax.ShapeDtypeStruct((HV, TOK, DK), F32),
        ],
        scratch_shapes=[
            pltpu.VMEM((heads, TOK, TOK), F32),
            pltpu.VMEM((heads, TOK, TOK), F32),
            pltpu.VMEM((heads, TOK, TOK), BF16),
        ],
        compiler_params=pltpu.CompilerParams(vmem_limit_bytes=40 << 20),
        name="local_terms",
    )(query, key, value, log_decay.reshape(GROUPS, heads, TOK), strength.reshape(GROUPS, heads, TOK))


def chain_kernel(map_ref, state_ref):
    count = map_ref.shape[0]

    def step(p, state):
        high, low = halves(state)
        state_ref[p] = high
        both = mul(jnp.concatenate([high, low], axis=0), map_ref[p, 0:128])
        parts = map_ref[p, 192:208].astype(F32)
        gamma = parts[0:1] + parts[1:2] + parts[2:3]
        return state * gamma + (both[:64] + both[64:]) + map_ref[p, 128:192].astype(F32)

    lax.fori_loop(0, count, step, jnp.zeros((64, DK), F32), unroll=4)


def chain(maps):
    count = maps.shape[0]
    return pl.pallas_call(
        chain_kernel,
        out_shape=jax.ShapeDtypeStruct((count, 64, DK), BF16),
        in_specs=[pl.BlockSpec(memory_space=pltpu.VMEM)],
        out_specs=pl.BlockSpec(memory_space=pltpu.VMEM),
        compiler_params=pltpu.CompilerParams(vmem_limit_bytes=40 << 20),
        name="chain",
    )(maps)


def finish_kernel(state_ref, reader_ref, local_ref, gate_ref, gain_ref, weight_ref, resid_ref, post_ref, mid_ref, moe_ref, normed_ref):
    step = pl.program_id(0)
    width = weight_ref.shape[1]

    @pl.when(step == 0)
    def _():
        for h in range(HV):
            kept = mul(reader_ref[h], state_ref[h], NT) + local_ref[h]
            scaled = kept * lax.rsqrt(jnp.mean(kept * kept, axis=-1, keepdims=True) + EPSILON)
            gate = gate_ref[:, h * DK:(h + 1) * DK].astype(F32)
            normed_ref[:, h * DK:(h + 1) * DK] = (
                scaled * gain_ref[...] * (gate / (1.0 + jnp.exp(-gate)))
            ).astype(BF16)

    lanes = pl.ds(pl.multiple_of(step * width, width), width)
    mid_ref[:, lanes] = resid_ref[:, lanes].astype(F32) + mul(normed_ref[...], weight_ref[...])

    @pl.when(step == pl.num_programs(0) - 1)
    def _():
        mid = mid_ref[...]
        moe_ref[...] = (
            mid * lax.rsqrt(jnp.mean(mid * mid, axis=-1, keepdims=True) + EPSILON) * post_ref[...]
        ).astype(BF16)


def finish(state, reader, local, gate, gain, weight, resid, post):
    depth, width = weight.shape
    tile = 512
    whole2 = lambda i: (0, 0)
    whole3 = lambda i: (0, 0, 0)
    return pl.pallas_call(
        finish_kernel,
        grid=(width // tile,),
        in_specs=[
            pl.BlockSpec((HV, DK, DK), whole3),
            pl.BlockSpec((HV, TOK, DK), whole3),
            pl.BlockSpec((HV, TOK, DK), whole3),
            pl.BlockSpec((TOK, HV * DK), whole2),
            pl.BlockSpec((1, DK), whole2),
            pl.BlockSpec((depth, tile), lambda i: (0, i)),
            pl.BlockSpec((TOK, width), whole2),
            pl.BlockSpec((1, width), whole2),
        ],
        out_specs=[pl.BlockSpec((TOK, width), whole2), pl.BlockSpec((TOK, width), whole2)],
        out_shape=[jax.ShapeDtypeStruct((TOK, width), F32), jax.ShapeDtypeStruct((TOK, width), BF16)],
        scratch_shapes=[pltpu.VMEM((TOK, HV * DK), BF16)],
        compiler_params=pltpu.CompilerParams(vmem_limit_bytes=40 << 20),
        name="finish",
    )(state, reader, local, gate, gain[None], weight, resid, post[None])


def expert_kernel(x_ref, up_ref, down_ref, y_ref):
    sources, _, width = x_ref.shape
    hidden_width = down_ref.shape[1]
    rows = sources * ROWS
    x = x_ref[...].astype(F32)
    results = []
    for j in range(2):
        mine = x[:, j * ROWS:(j + 1) * ROWS].reshape(rows, width).astype(BF16)
        gate = mul(mine, up_ref[j, :, :hidden_width])
        lift = mul(mine, up_ref[j, :, hidden_width:])
        hidden = (gate / (1.0 + jnp.exp(-gate)) * lift).astype(BF16)
        results.append(mul(hidden, down_ref[j]).reshape(sources, ROWS, width))
    y_ref[...] = jnp.concatenate(results, axis=1).astype(BF16)


def experts(x, up, down):
    count, rows, width = x.shape
    tile = 32
    whole3 = lambda i: (0, 0, 0)
    return pl.pallas_call(
        expert_kernel,
        grid=(count // tile,),
        in_specs=[
            pl.BlockSpec((tile, rows, width), lambda i: (i, 0, 0)),
            pl.BlockSpec(up.shape, whole3, pipeline_mode=pl.Buffered(1)),
            pl.BlockSpec(down.shape, whole3, pipeline_mode=pl.Buffered(1)),
        ],
        out_specs=pl.BlockSpec((tile, rows, width), lambda i: (i, 0, 0)),
        out_shape=jax.ShapeDtypeStruct(x.shape, BF16),
        compiler_params=pltpu.CompilerParams(vmem_limit_bytes=56 << 20),
        name="experts",
    )(x, up, down)


def shards(
    query_rows,
    key_rows,
    value_rows,
    gate_z,
    log_decay,
    write_strength,
    norm_gain,
    out_weight,
    residual,
    post_gain,
    expert_ids,
    gate_scores,
    expert_up,
    expert_down,
):
    width = residual.shape[2]
    devices = lax.axis_size("seq") * lax.axis_size("batch")
    exp_dev = expert_up.shape[0]
    total_experts = exp_dev * devices
    slots = total_experts * ROWS

    maps, reader, local = local_terms(
        query_rows[0], key_rows[0], value_rows[0], log_decay[0], write_strength[0]
    )
    maps = lax.all_to_all(maps, "seq", split_axis=0, concat_axis=0, tiled=True)
    states = chain(maps)
    states = lax.all_to_all(states, "seq", split_axis=0, concat_axis=0, tiled=True)
    mid, moe_in = finish(
        states.reshape(HV, DK, DK), reader, local, gate_z[0], norm_gain, out_weight, residual[0], post_gain
    )

    ids = expert_ids[0]
    scores = gate_scores[0]
    weights = scores / jnp.sum(scores, axis=-1, keepdims=True)
    named = ids.T[:, None, :] == jnp.arange(total_experts, dtype=jnp.int32)[None, :, None]
    chosen = jnp.sum(named.astype(F32), axis=0)
    share = jnp.sum(jnp.where(named, weights.T[:, None, :], 0.0), axis=0)
    earlier = jnp.triu(jnp.ones((TOK, TOK), BF16), 1)
    rank = jnp.dot(chosen.astype(BF16), earlier, preferred_element_type=F32)
    place = jnp.where(chosen > 0, rank, -1.0)
    pick = place[:, None, :] == jnp.arange(ROWS, dtype=F32)[None, :, None]
    take = pick.astype(BF16).reshape(slots, TOK)
    give = jnp.where(pick, share[:, None, :], 0.0).reshape(slots, TOK)
    give_high = give.astype(BF16)
    give_low = (give - give_high.astype(F32)).astype(BF16)

    outgoing = jnp.dot(take, moe_in, preferred_element_type=F32).astype(BF16)
    arrived = lax.all_to_all(
        outgoing.reshape(devices, exp_dev * ROWS, width), ("seq", "batch"), split_axis=0, concat_axis=0, tiled=True
    )
    result = experts(arrived, expert_up, expert_down)
    returned = lax.all_to_all(result, ("seq", "batch"), split_axis=0, concat_axis=0, tiled=True)
    returned = returned.reshape(slots, width)
    mixed = mid + (mul(give_high, returned, TN) + mul(give_low, returned, TN))
    return mixed.astype(BF16)[None]


def solution(mesh):
    return jax.shard_map(
        shards,
        mesh=mesh,
        in_specs=(
            P("batch", "seq", None),
            P("batch", "seq", None),
            P("batch", "seq", None),
            P("batch", "seq", None),
            P("batch", None, "seq"),
            P("batch", None, "seq"),
            P(),
            P(),
            P("batch", "seq", None),
            P(),
            P("batch", "seq", None),
            P("batch", "seq", None),
            P(("seq", "batch"), None, None),
            P(("seq", "batch"), None, None),
        ),
        out_specs=P("batch", "seq", None),
        check_vma=False,
    )
```

```python
import jax
import jax.numpy as jnp
from jax import lax
from jax.experimental import pallas as pl
from jax.experimental.pallas import tpu as pltpu
from jax.sharding import PartitionSpec as P

TOK = 128
DK = 128
HV = 16
HK = 8
GROUPS = 2
ROWS = 8
MSG = 272
VMEM = 60 << 20
MESH = pl.DeviceIdType.MESH
EPSILON = 1e-06
PRECISE = lax.Precision.HIGHEST
F32 = jnp.float32
BF16 = jnp.bfloat16

NN = (((1,), (0,)), ((), ()))
NT = (((1,), (1,)), ((), ()))
TN = (((0,), (0,)), ((), ()))


def mul(a, b, dims=NN):
    return lax.dot_general(a, b, dims, preferred_element_type=F32)


def mul_precise(a, b, dims=NN):
    return lax.dot_general(a, b, dims, preferred_element_type=F32, precision=PRECISE)


def halves(a):
    high = a.astype(BF16)
    return high, (a - high.astype(F32)).astype(BF16)


def local_kernel(q_ref, k_ref, v_ref, ld_ref, bt_ref, msg_ref, reader_ref, local_ref, n_ref, x_ref, s_ref):
    heads = HV // GROUPS
    row = lax.broadcasted_iota(jnp.int32, (TOK, TOK), 0)
    col = lax.broadcasted_iota(jnp.int32, (TOK, TOK), 1)
    ld = ld_ref[0]
    cum_row = mul_precise(ld, (row <= col).astype(F32))
    cum_col = mul_precise((row >= col).astype(F32), ld, NT)
    beta_col = bt_ref[0].T
    units = []
    for g in range(heads // 2):
        lanes = slice(g * DK, (g + 1) * DK)
        k_raw = k_ref[:, lanes]
        q_raw = q_ref[:, lanes]
        k_full = k_raw.astype(F32)
        q_full = q_raw.astype(F32)
        k_scale = lax.rsqrt(jnp.sum(k_full * k_full, axis=-1, keepdims=True) + EPSILON)
        q_scale = lax.rsqrt(jnp.sum(q_full * q_full, axis=-1, keepdims=True) + EPSILON) * DK ** (-0.5)
        k_unit = k_full * k_scale
        k_high, k_low = halves(k_unit)
        right = jnp.concatenate([k_high, k_low], axis=1)
        key_key = mul(jnp.concatenate([k_raw, k_raw], axis=1), right, NT) * k_scale
        query_key = mul(jnp.concatenate([q_raw, q_raw], axis=1), right, NT) * q_scale
        units.append((k_unit, q_full * q_scale))
        for h in (2 * g, 2 * g + 1):
            gap = cum_col[:, h:h + 1] - cum_row[h:h + 1, :]
            decay = jnp.where(row >= col, jnp.exp(jnp.minimum(gap, 0.0)), 0.0)
            s_ref[h] = (decay * query_key).astype(BF16)
            system = jnp.where(row > col, decay * key_key, 0.0) * beta_col[:, h:h + 1]
            n_ref[h] = system
            x_ref[h] = jnp.where((row ^ col) == 1, -system, 0.0)
    for level in range(1, 7):
        cross = ((row >> level) ^ (col >> level)) == 1
        left = []
        for h in range(heads):
            part = jnp.where(cross, n_ref[h], 0.0)
            left.append(part + mul(x_ref[h].astype(BF16), part.astype(BF16)))
        for h in range(heads):
            old = x_ref[h]
            x_ref[h] = old - left[h] - mul(left[h].astype(BF16), old.astype(BF16))
    for h in range(heads):
        k_unit, q_unit = units[h // 2]
        cum = cum_col[:, h:h + 1]
        last = cum_row[h:h + 1, TOK - 1:TOK]
        beta = beta_col[:, h:h + 1]
        gamma = jnp.exp(cum)
        value = v_ref[:, h * DK:(h + 1) * DK].astype(F32) * beta
        right = jnp.concatenate([value, k_unit * (beta * gamma)], axis=1)
        write = (right + mul(x_ref[h].astype(BF16), right.astype(BF16))).astype(BF16)
        tail = (jnp.exp(last - cum) * k_unit).astype(BF16)
        moved = mul(write, tail, TN)
        trans = (-moved[DK:]).astype(BF16)
        inject = moved[:DK].astype(BF16)
        read = mul(s_ref[h], write)
        local_ref[h] = read[:, :DK]
        reader_ref[h] = (gamma * q_unit - read[:, DK:]).astype(BF16)
        whole = jnp.exp(jnp.broadcast_to(last, (16, DK)))
        part0 = whole.astype(BF16)
        part1 = (whole - part0.astype(F32)).astype(BF16)
        part2 = (whole - part0.astype(F32) - part1.astype(F32)).astype(BF16)
        line = lax.broadcasted_iota(jnp.int32, (16, DK), 0)
        parts = jnp.where(line == 0, part0.astype(F32), jnp.where(line == 1, part1.astype(F32), part2.astype(F32)))
        parts = jnp.where(line < 3, parts, 0.0).astype(BF16)
        msg_ref[h, 0:128] = trans
        msg_ref[h, 128:256] = inject
        msg_ref[h, 256:272] = parts


def local_terms(query, key, value, log_decay, strength):
    heads = HV // GROUPS
    return pl.pallas_call(
        local_kernel,
        grid=(GROUPS,),
        in_specs=[
            pl.BlockSpec((TOK, heads // 2 * DK), lambda i: (0, i)),
            pl.BlockSpec((TOK, heads // 2 * DK), lambda i: (0, i)),
            pl.BlockSpec((TOK, heads * DK), lambda i: (0, i)),
            pl.BlockSpec((1, heads, TOK), lambda i: (i, 0, 0)),
            pl.BlockSpec((1, heads, TOK), lambda i: (i, 0, 0)),
        ],
        out_specs=[
            pl.BlockSpec((heads, MSG, DK), lambda i: (i, 0, 0)),
            pl.BlockSpec((heads, TOK, DK), lambda i: (i, 0, 0)),
            pl.BlockSpec((heads, TOK, DK), lambda i: (i, 0, 0)),
        ],
        out_shape=[
            jax.ShapeDtypeStruct((HV, MSG, DK), BF16),
            jax.ShapeDtypeStruct((HV, TOK, DK), BF16),
            jax.ShapeDtypeStruct((HV, TOK, DK), F32),
        ],
        scratch_shapes=[
            pltpu.VMEM((heads, TOK, TOK), F32),
            pltpu.VMEM((heads, TOK, TOK), F32),
            pltpu.VMEM((heads, TOK, TOK), BF16),
        ],
        compiler_params=pltpu.CompilerParams(vmem_limit_bytes=VMEM),
        name="local_terms",
    )(query, key, value, log_decay.reshape(GROUPS, heads, TOK), strength.reshape(GROUPS, heads, TOK))


PAIRS = (
    ((1, 1), (3, 3), (1, 3), (3, 1)),
    ((2, 2),),
    ((1, 0), (3, 0), (0, 1), (0, 3)),
    ((2, 0), (0, 2)),
    ((2, 1), (2, 3)),
    ((1, 2), (3, 2)),
)


def prefix_kernel(map_ref, state_ref, inbox, outbox, send, receive, send_back, receive_back):
    seq, batch = lax.axis_index("seq"), lax.axis_index("batch")
    z, x, core = seq // 8, seq // 2 % 4, seq % 2
    count = inbox.shape[0]
    head = z * 4 + x

    barrier = pltpu.get_barrier_semaphore()
    for other in range(1, count):
        pl.semaphore_signal(
            barrier, inc=1, device_id=(lax.rem(seq + other, count), batch), device_id_type=MESH
        )
    pl.semaphore_wait(barrier, count - 1)

    def to_owner(p, q):
        chip = lax.rem(z + p, 4) * 4 + lax.rem(x + q, 4)
        return pltpu.make_async_remote_copy(
            map_ref.at[chip], inbox.at[seq], send.at[p * 4 + q], receive.at[seq],
            device_id=(chip * 2, batch), device_id_type=MESH,
        )

    def own():
        return pltpu.make_async_copy(map_ref.at[head], inbox.at[seq], receive.at[seq])

    def back(place):
        return pltpu.make_async_remote_copy(
            outbox.at[place], state_ref.at[head], send_back.at[place], receive_back.at[head],
            device_id=(place, batch), device_id_type=MESH,
        )

    def own_back():
        return pltpu.make_async_copy(outbox.at[seq], state_ref.at[head], receive_back.at[head])

    far = [offset for group in PAIRS for offset in group]
    for p, q in far:
        to_owner(p, q).start()

    @pl.when(core == 1)
    def _():
        to_owner(0, 0).start()

    @pl.when(core == 0)
    def _():
        own().start()

        def step(place, state):
            pltpu.make_async_copy(inbox.at[place], inbox.at[place], receive.at[place]).wait()
            high, low = halves(state)
            outbox[place] = high

            @pl.when(place == seq)
            def _():
                own_back().start()

            @pl.when(place != seq)
            def _():
                back(place).start()

            both = mul(jnp.concatenate([high, low], axis=0), inbox[place, 0:128])
            parts = inbox[place, 256:272].astype(F32)
            gamma = parts[0:1] + parts[1:2] + parts[2:3]
            return state * gamma + (both[:DK] + both[DK:]) + inbox[place, 128:256].astype(F32)

        lax.fori_loop(0, count, step, jnp.zeros((DK, DK), F32))

        def sent(place, carry):
            @pl.when(place != seq)
            def _():
                back(place).wait_send()

            return carry

        lax.fori_loop(0, count, sent, 0)

    for p, q in far:
        to_owner(p, q).wait_send()

    @pl.when(core == 1)
    def _():
        to_owner(0, 0).wait_send()

    def arrived(place, carry):
        pltpu.make_async_copy(state_ref.at[place], state_ref.at[place], receive_back.at[place]).wait()
        return carry

    lax.fori_loop(0, HV, arrived, 0)


def prefix(maps, count):
    dma = pltpu.SemaphoreType.DMA
    return pl.pallas_call(
        prefix_kernel,
        out_shape=jax.ShapeDtypeStruct((HV, DK, DK), BF16),
        in_specs=[pl.BlockSpec(memory_space=pltpu.VMEM)],
        out_specs=pl.BlockSpec(memory_space=pltpu.VMEM),
        scratch_shapes=[
            pltpu.VMEM((count, MSG, DK), BF16),
            pltpu.VMEM((count, DK, DK), BF16),
            dma((HV,)),
            dma((count,)),
            dma((count,)),
            dma((HV,)),
        ],
        compiler_params=pltpu.CompilerParams(
            collective_id=0, has_side_effects=True, vmem_limit_bytes=VMEM
        ),
        name="prefix",
    )(maps)


def finish_kernel(state_ref, reader_ref, local_ref, gate_ref, gain_ref, weight_ref, resid_ref, post_ref, mid_ref, moe_ref, normed_ref):
    step = pl.program_id(0)
    width = weight_ref.shape[1]

    @pl.when(step == 0)
    def _():
        for h in range(HV):
            kept = mul(reader_ref[h], state_ref[h], NT) + local_ref[h]
            scaled = kept * lax.rsqrt(jnp.mean(kept * kept, axis=-1, keepdims=True) + EPSILON)
            gate = gate_ref[:, h * DK:(h + 1) * DK].astype(F32)
            normed_ref[:, h * DK:(h + 1) * DK] = (
                scaled * gain_ref[...] * (gate / (1.0 + jnp.exp(-gate)))
            ).astype(BF16)

    lanes = pl.ds(pl.multiple_of(step * width, width), width)
    mid_ref[:, lanes] = resid_ref[:, lanes].astype(F32) + mul(normed_ref[...], weight_ref[...])

    @pl.when(step == pl.num_programs(0) - 1)
    def _():
        mid = mid_ref[...]
        moe_ref[...] = (
            mid * lax.rsqrt(jnp.mean(mid * mid, axis=-1, keepdims=True) + EPSILON) * post_ref[...]
        ).astype(BF16)


def finish(state, reader, local, gate, gain, weight, resid, post):
    depth, width = weight.shape
    tile = 512
    whole2 = lambda i: (0, 0)
    whole3 = lambda i: (0, 0, 0)
    return pl.pallas_call(
        finish_kernel,
        grid=(width // tile,),
        in_specs=[
            pl.BlockSpec((HV, DK, DK), whole3),
            pl.BlockSpec((HV, TOK, DK), whole3),
            pl.BlockSpec((HV, TOK, DK), whole3),
            pl.BlockSpec((TOK, HV * DK), whole2),
            pl.BlockSpec((1, DK), whole2),
            pl.BlockSpec((depth, tile), lambda i: (0, i)),
            pl.BlockSpec((TOK, width), whole2),
            pl.BlockSpec((1, width), whole2),
        ],
        out_specs=[pl.BlockSpec((TOK, width), whole2), pl.BlockSpec((TOK, width), whole2)],
        out_shape=[jax.ShapeDtypeStruct((TOK, width), F32), jax.ShapeDtypeStruct((TOK, width), BF16)],
        scratch_shapes=[pltpu.VMEM((TOK, HV * DK), BF16)],
        compiler_params=pltpu.CompilerParams(vmem_limit_bytes=VMEM),
        name="finish",
    )(state, reader, local, gate, gain[None], weight, resid, post[None])


def expert_kernel(x_ref, up_ref, down_ref, y_ref):
    sources, _, width = x_ref.shape
    hidden_width = down_ref.shape[1]
    rows = sources * ROWS
    x = x_ref[...].astype(F32)
    results = []
    for j in range(2):
        mine = x[:, j * ROWS:(j + 1) * ROWS].reshape(rows, width).astype(BF16)
        gate = mul(mine, up_ref[j, :, :hidden_width])
        lift = mul(mine, up_ref[j, :, hidden_width:])
        hidden = (gate / (1.0 + jnp.exp(-gate)) * lift).astype(BF16)
        results.append(mul(hidden, down_ref[j]).reshape(sources, ROWS, width))
    y_ref[...] = jnp.concatenate(results, axis=1).astype(BF16)


def experts(x, up, down):
    count, rows, width = x.shape
    tile = 32
    whole3 = lambda i: (0, 0, 0)
    return pl.pallas_call(
        expert_kernel,
        grid=(count // tile,),
        in_specs=[
            pl.BlockSpec((tile, rows, width), lambda i: (i, 0, 0)),
            pl.BlockSpec(up.shape, whole3, pipeline_mode=pl.Buffered(1)),
            pl.BlockSpec(down.shape, whole3, pipeline_mode=pl.Buffered(1)),
        ],
        out_specs=pl.BlockSpec((tile, rows, width), lambda i: (i, 0, 0)),
        out_shape=jax.ShapeDtypeStruct(x.shape, BF16),
        compiler_params=pltpu.CompilerParams(vmem_limit_bytes=VMEM),
        name="experts",
    )(x, up, down)


def shards(
    query_rows,
    key_rows,
    value_rows,
    gate_z,
    log_decay,
    write_strength,
    norm_gain,
    out_weight,
    residual,
    post_gain,
    expert_ids,
    gate_scores,
    expert_up,
    expert_down,
):
    width = residual.shape[2]
    devices = lax.axis_size("seq") * lax.axis_size("batch")
    exp_dev = expert_up.shape[0]
    total_experts = exp_dev * devices
    slots = total_experts * ROWS

    maps, reader, local = local_terms(
        query_rows[0], key_rows[0], value_rows[0], log_decay[0], write_strength[0]
    )
    states = prefix(maps, lax.axis_size("seq"))
    mid, moe_in = finish(
        states, reader, local, gate_z[0], norm_gain, out_weight, residual[0], post_gain
    )

    ids = expert_ids[0]
    scores = gate_scores[0]
    weights = scores / jnp.sum(scores, axis=-1, keepdims=True)
    named = ids.T[:, None, :] == jnp.arange(total_experts, dtype=jnp.int32)[None, :, None]
    chosen = jnp.sum(named.astype(F32), axis=0)
    share = jnp.sum(jnp.where(named, weights.T[:, None, :], 0.0), axis=0)
    earlier = jnp.triu(jnp.ones((TOK, TOK), BF16), 1)
    rank = jnp.dot(chosen.astype(BF16), earlier, preferred_element_type=F32)
    place = jnp.where(chosen > 0, rank, -1.0)
    pick = place[:, None, :] == jnp.arange(ROWS, dtype=F32)[None, :, None]
    take = pick.astype(BF16).reshape(slots, TOK)
    give = jnp.where(pick, share[:, None, :], 0.0).reshape(slots, TOK)
    give_high = give.astype(BF16)
    give_low = (give - give_high.astype(F32)).astype(BF16)

    outgoing = jnp.dot(take, moe_in, preferred_element_type=F32).astype(BF16)
    arrived = lax.all_to_all(
        outgoing.reshape(devices, exp_dev * ROWS, width), ("seq", "batch"), split_axis=0, concat_axis=0, tiled=True
    )
    result = experts(arrived, expert_up, expert_down)
    returned = lax.all_to_all(result, ("seq", "batch"), split_axis=0, concat_axis=0, tiled=True)
    returned = returned.reshape(slots, width)
    mixed = mid + (mul(give_high, returned, TN) + mul(give_low, returned, TN))
    return mixed.astype(BF16)[None]


def solution(mesh):
    return jax.shard_map(
        shards,
        mesh=mesh,
        in_specs=(
            P("batch", "seq", None),
            P("batch", "seq", None),
            P("batch", "seq", None),
            P("batch", "seq", None),
            P("batch", None, "seq"),
            P("batch", None, "seq"),
            P(),
            P(),
            P("batch", "seq", None),
            P(),
            P("batch", "seq", None),
            P("batch", "seq", None),
            P(("seq", "batch"), None, None),
            P(("seq", "batch"), None, None),
        ),
        out_specs=P("batch", "seq", None),
        check_vma=False,
    )
```

```python
import functools

import jax
import jax.numpy as jnp
from jax import lax
from jax.experimental import pallas as pl
from jax.experimental.pallas import tpu as pltpu
from jax.sharding import PartitionSpec as P

TOK = 128
DK = 128
HV = 16
HK = 8
GROUPS = 2
ROWS = 8
MSG = 272
VMEM = 60 << 20
PARTS = ((0, 768), (768, 1408), (1408, 2048))
MESH = pl.DeviceIdType.MESH
EPSILON = 1e-06
PRECISE = lax.Precision.HIGHEST
F32 = jnp.float32
BF16 = jnp.bfloat16

NN = (((1,), (0,)), ((), ()))
NT = (((1,), (1,)), ((), ()))
TN = (((0,), (0,)), ((), ()))


def mul(a, b, dims=NN):
    return lax.dot_general(a, b, dims, preferred_element_type=F32)


def mul_precise(a, b, dims=NN):
    return lax.dot_general(a, b, dims, preferred_element_type=F32, precision=PRECISE)


def halves(a):
    high = a.astype(BF16)
    return high, (a - high.astype(F32)).astype(BF16)


def local_kernel(q_ref, k_ref, v_ref, ld_ref, bt_ref, msg_ref, reader_ref, local_ref, n_ref, x_ref, s_ref):
    heads = HV // GROUPS
    row = lax.broadcasted_iota(jnp.int32, (TOK, TOK), 0)
    col = lax.broadcasted_iota(jnp.int32, (TOK, TOK), 1)
    ld = ld_ref[0]
    cum_row = mul_precise(ld, (row <= col).astype(F32))
    cum_col = mul_precise((row >= col).astype(F32), ld, NT)
    beta_col = bt_ref[0].T
    units = []
    for g in range(heads // 2):
        lanes = slice(g * DK, (g + 1) * DK)
        k_raw = k_ref[:, lanes]
        q_raw = q_ref[:, lanes]
        k_full = k_raw.astype(F32)
        q_full = q_raw.astype(F32)
        k_scale = lax.rsqrt(jnp.sum(k_full * k_full, axis=-1, keepdims=True) + EPSILON)
        q_scale = lax.rsqrt(jnp.sum(q_full * q_full, axis=-1, keepdims=True) + EPSILON) * DK ** (-0.5)
        k_unit = k_full * k_scale
        k_high, k_low = halves(k_unit)
        right = jnp.concatenate([k_high, k_low], axis=1)
        key_key = mul(jnp.concatenate([k_raw, k_raw], axis=1), right, NT) * k_scale
        query_key = mul(jnp.concatenate([q_raw, q_raw], axis=1), right, NT) * q_scale
        units.append((k_unit, q_full * q_scale))
        for h in (2 * g, 2 * g + 1):
            gap = cum_col[:, h:h + 1] - cum_row[h:h + 1, :]
            decay = jnp.where(row >= col, jnp.exp(jnp.minimum(gap, 0.0)), 0.0)
            s_ref[h] = (decay * query_key).astype(BF16)
            system = jnp.where(row > col, decay * key_key, 0.0) * beta_col[:, h:h + 1]
            n_ref[h] = system
            x_ref[h] = jnp.where((row ^ col) == 1, -system, 0.0)
    for level in range(1, 7):
        cross = ((row >> level) ^ (col >> level)) == 1
        left = []
        for h in range(heads):
            part = jnp.where(cross, n_ref[h], 0.0)
            left.append(part + mul(x_ref[h].astype(BF16), part.astype(BF16)))
        for h in range(heads):
            old = x_ref[h]
            x_ref[h] = old - left[h] - mul(left[h].astype(BF16), old.astype(BF16))
    for h in range(heads):
        k_unit, q_unit = units[h // 2]
        cum = cum_col[:, h:h + 1]
        last = cum_row[h:h + 1, TOK - 1:TOK]
        beta = beta_col[:, h:h + 1]
        gamma = jnp.exp(cum)
        value = v_ref[:, h * DK:(h + 1) * DK].astype(F32) * beta
        right = jnp.concatenate([value, k_unit * (beta * gamma)], axis=1)
        write = (right + mul(x_ref[h].astype(BF16), right.astype(BF16))).astype(BF16)
        tail = (jnp.exp(last - cum) * k_unit).astype(BF16)
        moved = mul(write, tail, TN)
        trans = (-moved[DK:]).astype(BF16)
        inject = moved[:DK].astype(BF16)
        read = mul(s_ref[h], write)
        local_ref[h] = read[:, :DK]
        reader_ref[h] = (gamma * q_unit - read[:, DK:]).astype(BF16)
        whole = jnp.exp(jnp.broadcast_to(last, (16, DK)))
        part0 = whole.astype(BF16)
        part1 = (whole - part0.astype(F32)).astype(BF16)
        part2 = (whole - part0.astype(F32) - part1.astype(F32)).astype(BF16)
        line = lax.broadcasted_iota(jnp.int32, (16, DK), 0)
        parts = jnp.where(line == 0, part0.astype(F32), jnp.where(line == 1, part1.astype(F32), part2.astype(F32)))
        parts = jnp.where(line < 3, parts, 0.0).astype(BF16)
        msg_ref[h, 0:128] = trans
        msg_ref[h, 128:256] = inject
        msg_ref[h, 256:272] = parts


def local_terms(query, key, value, log_decay, strength):
    heads = HV // GROUPS
    return pl.pallas_call(
        local_kernel,
        grid=(GROUPS,),
        in_specs=[
            pl.BlockSpec((TOK, heads // 2 * DK), lambda i: (0, i)),
            pl.BlockSpec((TOK, heads // 2 * DK), lambda i: (0, i)),
            pl.BlockSpec((TOK, heads * DK), lambda i: (0, i)),
            pl.BlockSpec((1, heads, TOK), lambda i: (i, 0, 0)),
            pl.BlockSpec((1, heads, TOK), lambda i: (i, 0, 0)),
        ],
        out_specs=[
            pl.BlockSpec((heads, MSG, DK), lambda i: (i, 0, 0)),
            pl.BlockSpec((heads, TOK, DK), lambda i: (i, 0, 0)),
            pl.BlockSpec((heads, TOK, DK), lambda i: (i, 0, 0)),
        ],
        out_shape=[
            jax.ShapeDtypeStruct((HV, MSG, DK), BF16),
            jax.ShapeDtypeStruct((HV, TOK, DK), BF16),
            jax.ShapeDtypeStruct((HV, TOK, DK), F32),
        ],
        scratch_shapes=[
            pltpu.VMEM((heads, TOK, TOK), F32),
            pltpu.VMEM((heads, TOK, TOK), F32),
            pltpu.VMEM((heads, TOK, TOK), BF16),
        ],
        compiler_params=pltpu.CompilerParams(vmem_limit_bytes=VMEM),
        name="local_terms",
    )(query, key, value, log_decay.reshape(GROUPS, heads, TOK), strength.reshape(GROUPS, heads, TOK))


def axis_names():
    seq = lax.axis_index("seq")
    return (lax.div(seq, 8), lax.rem(lax.div(seq, 2), 4), lax.rem(seq, 2), lax.axis_index("batch"))


def device_at(offset):
    z, x, core, y = axis_names()
    dz, dx, dcore, dy = offset
    seq = lax.rem(z + dz, 4) * 8 + lax.rem(x + dx, 4) * 2 + lax.rem(core + dcore, 2)
    return (seq, lax.rem(y + dy, 4))


def greet(offsets):
    barrier = pltpu.get_barrier_semaphore()
    for offset in offsets:
        pl.semaphore_signal(barrier, inc=1, device_id=device_at(offset), device_id_type=MESH)
    pl.semaphore_wait(barrier, len(offsets))


def along(part, d):
    return ((0, 0, 0, d), (0, d, 0, 0), (d, 0, 0, 0))[part]


def across(part, p, q, dcore):
    return ((p, q, dcore, 0), (p, 0, dcore, q), (0, p, dcore, q))[part]


def line_place(part):
    z, x, _, y = axis_names()
    return (y, x, z)[part]


def plane_index(part, offset):
    z, x, core, y = axis_names()
    dz, dx, dcore, dy = offset
    z, x, y = lax.rem(z + dz, 4), lax.rem(x + dx, 4), lax.rem(y + dy, 4)
    first, second = ((z, x), (z, y), (x, y))[part]
    return (first * 4 + second) * 2 + lax.rem(core + dcore, 2)


PAIRS = (
    ((1, 1), (3, 3), (1, 3), (3, 1)),
    ((2, 2),),
    ((1, 0), (3, 0), (0, 1), (0, 3)),
    ((2, 0), (0, 2)),
    ((2, 1), (2, 3)),
    ((1, 2), (3, 2)),
)


def line_copies(sources, targets, semaphores, scatter):
    send, receive, own = semaphores
    copies = []
    for part in range(3):
        place = line_place(part)
        source = sources[part].at[place] if scatter else sources[part]
        copies.append(pltpu.make_async_copy(source, targets[part].at[place], own.at[part]))
    for d in (1, 3, 2):
        for part in range(3):
            place = line_place(part)
            source = sources[part].at[lax.rem(place + d, 4)] if scatter else sources[part]
            copies.append(pltpu.make_async_remote_copy(
                source, targets[part].at[place], send.at[part, d], receive.at[part, d],
                device_id=device_at(along(part, d)), device_id_type=MESH,
            ))
    return copies


def prefix_kernel(map_ref, table_ref, state_ref, tables_ref, inbox, outbox, send, receive, send_back, receive_back, *lines):
    seq, batch = lax.axis_index("seq"), lax.axis_index("batch")
    z, x, core = seq // 8, seq // 2 % 4, seq % 2
    count = inbox.shape[0]
    head = z * 4 + x

    barrier = pltpu.get_barrier_semaphore()
    for other in range(1, count):
        pl.semaphore_signal(
            barrier, inc=1, device_id=(lax.rem(seq + other, count), batch), device_id_type=MESH
        )
    for d in (1, 2, 3):
        pl.semaphore_signal(barrier, inc=1, device_id=device_at((0, 0, 0, d)), device_id_type=MESH)
    pl.semaphore_wait(barrier, count + 2)
    tables = line_copies((table_ref,) * 3, [tables_ref.at[part] for part in range(3)], lines, False)
    for copy in tables:
        copy.start()

    def to_owner(p, q):
        chip = lax.rem(z + p, 4) * 4 + lax.rem(x + q, 4)
        return pltpu.make_async_remote_copy(
            map_ref.at[chip], inbox.at[seq], send.at[p * 4 + q], receive.at[seq],
            device_id=(chip * 2, batch), device_id_type=MESH,
        )

    def own():
        return pltpu.make_async_copy(map_ref.at[head], inbox.at[seq], receive.at[seq])

    def back(place):
        return pltpu.make_async_remote_copy(
            outbox.at[place], state_ref.at[head], send_back.at[place], receive_back.at[head],
            device_id=(place, batch), device_id_type=MESH,
        )

    def own_back():
        return pltpu.make_async_copy(outbox.at[seq], state_ref.at[head], receive_back.at[head])

    far = [offset for group in PAIRS for offset in group]
    for p, q in far:
        to_owner(p, q).start()

    @pl.when(core == 1)
    def _():
        to_owner(0, 0).start()

    @pl.when(core == 0)
    def _():
        own().start()

        def step(place, state):
            pltpu.make_async_copy(inbox.at[place], inbox.at[place], receive.at[place]).wait()
            high, low = halves(state)
            outbox[place] = high

            @pl.when(place == seq)
            def _():
                own_back().start()

            @pl.when(place != seq)
            def _():
                back(place).start()

            both = mul(jnp.concatenate([high, low], axis=0), inbox[place, 0:128])
            parts = inbox[place, 256:272].astype(F32)
            gamma = parts[0:1] + parts[1:2] + parts[2:3]
            return state * gamma + (both[:DK] + both[DK:]) + inbox[place, 128:256].astype(F32)

        lax.fori_loop(0, count, step, jnp.zeros((DK, DK), F32))

        def sent(place, carry):
            @pl.when(place != seq)
            def _():
                back(place).wait_send()

            return carry

        lax.fori_loop(0, count, sent, 0)

    for p, q in far:
        to_owner(p, q).wait_send()

    @pl.when(core == 1)
    def _():
        to_owner(0, 0).wait_send()

    def arrived(place, carry):
        pltpu.make_async_copy(state_ref.at[place], state_ref.at[place], receive_back.at[place]).wait()
        return carry

    lax.fori_loop(0, HV, arrived, 0)
    for copy in tables:
        copy.wait()


def prefix(maps, table, count):
    dma = pltpu.SemaphoreType.DMA
    return pl.pallas_call(
        prefix_kernel,
        out_shape=[
            jax.ShapeDtypeStruct((HV, DK, DK), BF16),
            jax.ShapeDtypeStruct((3, 4) + table.shape, BF16),
        ],
        in_specs=[pl.BlockSpec(memory_space=pltpu.VMEM)] * 2,
        out_specs=[pl.BlockSpec(memory_space=pltpu.VMEM)] * 2,
        scratch_shapes=[
            pltpu.VMEM((count, MSG, DK), BF16),
            pltpu.VMEM((count, DK, DK), BF16),
            dma((HV,)),
            dma((count,)),
            dma((count,)),
            dma((HV,)),
            dma((3, 4)),
            dma((3, 4)),
            dma((3,)),
        ],
        compiler_params=pltpu.CompilerParams(
            collective_id=0, has_side_effects=True, vmem_limit_bytes=VMEM
        ),
        name="prefix",
    )(maps, table)


def finish_kernel(state_ref, reader_ref, local_ref, gate_ref, gain_ref, weight_ref, resid_ref, post_ref, mid_ref, a_ref, b_ref, c_ref, normed_ref):
    step = pl.program_id(0)
    width = weight_ref.shape[1]

    @pl.when(step == 0)
    def _():
        for h in range(HV):
            kept = mul(reader_ref[h], state_ref[h], NT) + local_ref[h]
            scaled = kept * lax.rsqrt(jnp.mean(kept * kept, axis=-1, keepdims=True) + EPSILON)
            gate = gate_ref[:, h * DK:(h + 1) * DK].astype(F32)
            normed_ref[:, h * DK:(h + 1) * DK] = (
                scaled * gain_ref[...] * (gate / (1.0 + jnp.exp(-gate)))
            ).astype(BF16)

    lanes = pl.ds(pl.multiple_of(step * width, width), width)
    mid_ref[:, lanes] = resid_ref[:, lanes].astype(F32) + mul(normed_ref[...], weight_ref[...])

    @pl.when(step == pl.num_programs(0) - 1)
    def _():
        mid = mid_ref[...]
        moe_in = (
            mid * lax.rsqrt(jnp.mean(mid * mid, axis=-1, keepdims=True) + EPSILON) * post_ref[...]
        ).astype(BF16)
        for ref, (low, high) in zip((a_ref, b_ref, c_ref), PARTS):
            ref[...] = moe_in[:, low:high]


def finish(state, reader, local, gate, gain, weight, resid, post):
    depth, width = weight.shape
    tile = 512
    whole2 = lambda i: (0, 0)
    whole3 = lambda i: (0, 0, 0)
    return pl.pallas_call(
        finish_kernel,
        grid=(width // tile,),
        in_specs=[
            pl.BlockSpec((HV, DK, DK), whole3),
            pl.BlockSpec((HV, TOK, DK), whole3),
            pl.BlockSpec((HV, TOK, DK), whole3),
            pl.BlockSpec((TOK, HV * DK), whole2),
            pl.BlockSpec((1, DK), whole2),
            pl.BlockSpec((depth, tile), lambda i: (0, i)),
            pl.BlockSpec((TOK, width), whole2),
            pl.BlockSpec((1, width), whole2),
        ],
        out_specs=[pl.BlockSpec((TOK, width), whole2)]
        + [pl.BlockSpec((TOK, high - low), whole2) for low, high in PARTS],
        out_shape=[jax.ShapeDtypeStruct((TOK, width), F32)]
        + [jax.ShapeDtypeStruct((TOK, high - low), BF16) for low, high in PARTS],
        scratch_shapes=[pltpu.VMEM((TOK, HV * DK), BF16)],
        compiler_params=pltpu.CompilerParams(vmem_limit_bytes=VMEM),
        name="finish",
    )(state, reader, local, gate, gain[None], weight, resid, post[None])


ORDER = [(p, q, dcore) for group in PAIRS for dcore in (0, 1) for p, q in group] + [(0, 0, 1), (0, 0, 0)]


def plane_copy(source, target, send, receive, part, step):
    p, q, dcore = step
    offset = across(part, p, q, dcore)
    slot = p * 8 + q * 2 + dcore
    if step == (0, 0, 0):
        return pltpu.make_async_copy(source, target, receive.at[part, slot])
    return pltpu.make_async_remote_copy(
        source, target, send.at[part, slot], receive.at[part, slot],
        device_id=device_at(offset), device_id_type=MESH,
    )


def wait_sent(copy, step):
    if step != (0, 0, 0):
        copy.wait_send()


def wait_arrived(copy, step):
    if step == (0, 0, 0):
        copy.wait()
    else:
        copy.wait_recv()


def plane_offsets():
    return sorted(set(across(part, *step) for part in range(3) for step in ORDER) - {(0, 0, 0, 0)})


def picked(slot):
    rows = lax.broadcasted_iota(jnp.int32, (ROWS, TOK), 0).astype(F32)
    return slot[..., None, :] == rows


def dispatch_kernel(*refs):
    slot_ref, rows, outs = refs[0], refs[1:4], refs[4:7]
    lines, stages = refs[7:10], refs[10:13]
    line_semaphores, (send, receive) = refs[13:16], refs[16:18]
    greet(plane_offsets())
    gathers = line_copies(rows, lines, line_semaphores, False)
    for copy in gathers:
        copy.start()
    for copy in gathers:
        copy.wait()
    copies = []
    for g in range(4):
        steps = ORDER[8 * g:8 * g + 8]
        for part in range(3):
            places = [plane_index(part, across(part, *step)) for step in steps]

            def fill(a, carry, part=part, places=places, g=g):
                slots = jnp.concatenate([slot_ref[part, place, a] for place in places], axis=0)
                take = jnp.where(picked(slots), 1.0, 0.0).reshape(16 * ROWS, TOK).astype(BF16)
                packed = mul(take, lines[part][a]).astype(BF16)
                stages[part][8 * g:8 * g + 8, a] = packed.reshape(8, 2 * ROWS, packed.shape[1])
                return carry

            lax.fori_loop(0, 4, fill, 0)
            here = plane_index(part, (0, 0, 0, 0))
            for i, step in enumerate(steps):
                copy = plane_copy(stages[part].at[8 * g + i], outs[part].at[here], send, receive, part, step)
                copy.start()
                copies.append((copy, step))
    for copy, step in copies:
        wait_sent(copy, step)
        wait_arrived(copy, step)


def dispatch(slots, rows):
    dma = pltpu.SemaphoreType.DMA
    shapes = [(32, 4, 2 * ROWS, part.shape[1]) for part in rows]
    return pl.pallas_call(
        dispatch_kernel,
        in_specs=[pl.BlockSpec(memory_space=pltpu.VMEM)] * 4,
        out_specs=[pl.BlockSpec(memory_space=pl.ANY)] * 3,
        out_shape=[jax.ShapeDtypeStruct(shape, BF16) for shape in shapes],
        scratch_shapes=[pltpu.VMEM((4,) + part.shape, BF16) for part in rows]
        + [pltpu.VMEM(shape, BF16) for shape in shapes]
        + [dma((3, 4)), dma((3, 4)), dma((3,)), dma((3, 32)), dma((3, 32))],
        compiler_params=pltpu.CompilerParams(
            collective_id=1, has_side_effects=True, vmem_limit_bytes=VMEM
        ),
        name="dispatch",
    )(slots, *rows)


def collect_kernel(*refs):
    slot_ref, share_ref, mid_ref, results, out_ref = refs[0], refs[1], refs[2], refs[3:6], refs[6]
    landed, partials, sums = refs[7:10], refs[10:13], refs[13:16]
    send, receive = refs[16:18]
    line_semaphores = refs[18:21]
    greet(plane_offsets())
    copies = [[], [], []]
    for step in ORDER:
        for part in range(3):
            target = landed[part].at[plane_index(part, (0, 0, 0, 0))]
            source = results[part].at[plane_index(part, across(part, *step))]
            copy = plane_copy(source, target, send, receive, part, step)
            copy.start()
            copies[part].append((copy, step))
    lines = line_copies(partials, sums, line_semaphores, True)
    own, others = lines[0:3], lines[3:]
    for part in range(3):
        for copy, step in copies[part]:
            wait_arrived(copy, step)
        width = landed[part].shape[3]
        for n, d in enumerate((1, 3, 2, 0)):
            a = lax.rem(line_place(part) + d, 4)
            slot = slot_ref[part, :, a]
            give = jnp.where(picked(slot), share_ref[part, :, a][:, :, None, :], 0.0)
            high, low = halves(give.reshape(64 * ROWS, TOK))
            rows = landed[part][:, a].reshape(64 * ROWS, width)
            both = mul(jnp.concatenate([high, low], axis=1), rows, TN)
            partials[part][a] = (both[:TOK] + both[TOK:]).astype(BF16)
            copy = own[part] if d == 0 else others[3 * n + part]
            copy.start()
    for part, (low, high) in enumerate(PARTS):
        for n in range(3):
            others[3 * n + part].wait()
        own[part].wait()
        total = mid_ref[:, low:high]
        for a in range(4):
            total = total + sums[part][a].astype(F32)
        out_ref[:, low:high] = total.astype(BF16)
    for part in range(3):
        for copy, step in copies[part]:
            wait_sent(copy, step)


def collect(slots, shares, mid, results):
    dma = pltpu.SemaphoreType.DMA
    widths = [part.shape[3] for part in results]
    return pl.pallas_call(
        collect_kernel,
        in_specs=[pl.BlockSpec(memory_space=pltpu.VMEM)] * 3 + [pl.BlockSpec(memory_space=pl.ANY)] * 3,
        out_specs=pl.BlockSpec(memory_space=pltpu.VMEM),
        out_shape=jax.ShapeDtypeStruct(mid.shape, BF16),
        scratch_shapes=[pltpu.VMEM(part.shape, BF16) for part in results]
        + [pltpu.VMEM((4, TOK, width), BF16) for width in widths] * 2
        + [dma((3, 32)), dma((3, 32)), dma((3, 4)), dma((3, 4)), dma((3,))],
        compiler_params=pltpu.CompilerParams(
            collective_id=2, has_side_effects=True, vmem_limit_bytes=VMEM
        ),
        name="collect",
    )(slots, shares, mid, *results)


def part_views(parts):
    a, b, c = parts
    return (
        a.reshape(4, 4, 2, 4, 2 * ROWS, a.shape[3]),
        b.reshape(4, 4, 2, 4, 2 * ROWS, b.shape[3]),
        c.reshape(4, 4, 2, 4, 2 * ROWS, c.shape[3]),
    )


def expert_kernel(a_ref, b_ref, c_ref, up_ref, down_ref, ya_ref, yb_ref, yc_ref, x_ref, y_ref):
    hidden_width = down_ref.shape[1]
    wa, wb = a_ref.shape[5], b_ref.shape[5]
    width = x_ref.shape[2]
    sources = [(x * 8 + core * 4 + y, x, core, y) for x in range(4) for core in range(2) for y in range(4)]
    for n, x, core, y in sources:
        x_ref[n, :, 0:wa] = a_ref[0, x, core, y]
        x_ref[n, :, wa:wa + wb] = b_ref[0, y, core, x]
        x_ref[n, :, wa + wb:] = c_ref[x, y, core, 0]
    rows = len(sources) * ROWS
    x_all = x_ref[...].astype(F32)
    results = []
    for j in range(2):
        mine = x_all[:, j * ROWS:(j + 1) * ROWS].reshape(rows, width).astype(BF16)
        gate = mul(mine, up_ref[j, :, :hidden_width])
        lift = mul(mine, up_ref[j, :, hidden_width:])
        hidden = (gate / (1.0 + jnp.exp(-gate)) * lift).astype(BF16)
        results.append(mul(hidden, down_ref[j]).reshape(len(sources), ROWS, width))
    y_ref[...] = jnp.concatenate(results, axis=1).astype(BF16)
    for n, x, core, y in sources:
        ya_ref[0, x, core, y] = y_ref[n, :, 0:wa]
        yb_ref[0, y, core, x] = y_ref[n, :, wa:wa + wb]
        yc_ref[x, y, core, 0] = y_ref[n, :, wa + wb:]


def experts(parts, up, down):
    views = part_views(parts)
    width = up.shape[1]
    whole3 = lambda z: (0, 0, 0)
    first = lambda z: (z, 0, 0, 0, 0, 0)
    last = lambda z: (0, 0, 0, z, 0, 0)
    specs = [
        pl.BlockSpec((1,) + views[0].shape[1:], first),
        pl.BlockSpec((1,) + views[1].shape[1:], first),
        pl.BlockSpec(views[2].shape[:3] + (1,) + views[2].shape[4:], last),
    ]
    results = pl.pallas_call(
        expert_kernel,
        grid=(4,),
        in_specs=specs + [
            pl.BlockSpec(up.shape, whole3, pipeline_mode=pl.Buffered(1)),
            pl.BlockSpec(down.shape, whole3, pipeline_mode=pl.Buffered(1)),
        ],
        out_specs=specs,
        out_shape=[jax.ShapeDtypeStruct(view.shape, BF16) for view in views],
        scratch_shapes=[pltpu.VMEM((32, 2 * ROWS, width), BF16), pltpu.VMEM((32, 2 * ROWS, width), BF16)],
        compiler_params=pltpu.CompilerParams(vmem_limit_bytes=VMEM),
        name="experts",
    )(*views, up, down)
    return [result.reshape(part.shape) for result, part in zip(results, parts)]


def routing_table(ids, weights):
    high, low = halves(weights)
    return jnp.concatenate([ids.T.astype(BF16), high.T, low.T, jnp.zeros((2, TOK), BF16)], axis=0)


def routes(tables, top, exp_dev):
    z, x, core, y = axis_names()
    place = jnp.arange(32, dtype=jnp.int32)
    first, second, side = place // 8, place // 2 % 4, place % 2
    device = jnp.stack([
        place * 4 + y,
        (first * 8 + x * 2 + side) * 4 + second,
        (z * 8 + first * 2 + side) * 4 + second,
    ])
    numbers = tables[:, :, 0:top].astype(F32)
    share = tables[:, :, top:2 * top].astype(F32) + tables[:, :, 2 * top:3 * top].astype(F32)
    expert = (device[:, :, None] * exp_dev + jnp.arange(exp_dev)).astype(F32)
    named = numbers[:, None, :, None] == expert[:, :, None, :, None, None]
    chosen = jnp.sum(named.astype(F32), axis=4)
    given = jnp.sum(jnp.where(named, share[:, None, :, None], 0.0), axis=4)
    earlier = jnp.triu(jnp.ones((TOK, TOK), BF16), 1)
    rank = mul(chosen.astype(BF16).reshape(-1, TOK), earlier).reshape(chosen.shape)
    return jnp.where(chosen > 0, rank, -1.0), given


def shards(
    query_rows,
    key_rows,
    value_rows,
    gate_z,
    log_decay,
    write_strength,
    norm_gain,
    out_weight,
    residual,
    post_gain,
    expert_ids,
    gate_scores,
    expert_up,
    expert_down,
):
    exp_dev = expert_up.shape[0]
    scores = gate_scores[0]
    weights = scores / jnp.sum(scores, axis=-1, keepdims=True)
    table = routing_table(expert_ids[0], weights)
    maps, reader, local = local_terms(
        query_rows[0], key_rows[0], value_rows[0], log_decay[0], write_strength[0]
    )
    states, tables = prefix(maps, table, lax.axis_size("seq"))
    mid, *rows = finish(
        states, reader, local, gate_z[0], norm_gain, out_weight, residual[0], post_gain
    )
    slots, shares = routes(tables, expert_ids.shape[2], exp_dev)
    arrived = dispatch(slots, rows)
    results = experts(arrived, expert_up, expert_down)
    return collect(slots, shares, mid, results)[None]


def solution(mesh):
    return jax.shard_map(
        shards,
        mesh=mesh,
        in_specs=(
            P("batch", "seq", None),
            P("batch", "seq", None),
            P("batch", "seq", None),
            P("batch", "seq", None),
            P("batch", None, "seq"),
            P("batch", None, "seq"),
            P(),
            P(),
            P("batch", "seq", None),
            P(),
            P("batch", "seq", None),
            P("batch", "seq", None),
            P(("seq", "batch"), None, None),
            P(("seq", "batch"), None, None),
        ),
        out_specs=P("batch", "seq", None),
        check_vma=False,
    )
```

```python
import functools

import jax
import jax.numpy as jnp
from jax import lax
from jax.experimental import pallas as pl
from jax.experimental.pallas import tpu as pltpu
from jax.sharding import PartitionSpec as P

TOK = 128
DK = 128
HV = 16
HK = 8
GROUPS = 2
ROWS = 8
MSG = 272
VMEM = 60 << 20
PARTS = ((0, 768), (768, 1408), (1408, 2048))
MESH = pl.DeviceIdType.MESH
EPSILON = 1e-06
PRECISE = lax.Precision.HIGHEST
F32 = jnp.float32
BF16 = jnp.bfloat16

NN = (((1,), (0,)), ((), ()))
NT = (((1,), (1,)), ((), ()))
TN = (((0,), (0,)), ((), ()))


def mul(a, b, dims=NN):
    return lax.dot_general(a, b, dims, preferred_element_type=F32)


def mul_precise(a, b, dims=NN):
    return lax.dot_general(a, b, dims, preferred_element_type=F32, precision=PRECISE)


def halves(a):
    high = a.astype(BF16)
    return high, (a - high.astype(F32)).astype(BF16)


def local_kernel(q_ref, k_ref, v_ref, ld_ref, bt_ref, msg_ref, reader_ref, local_ref, n_ref, x_ref, s_ref):
    heads = HV // GROUPS
    row = lax.broadcasted_iota(jnp.int32, (TOK, TOK), 0)
    col = lax.broadcasted_iota(jnp.int32, (TOK, TOK), 1)
    ld = ld_ref[0]
    cum_row = mul_precise(ld, (row <= col).astype(F32))
    cum_col = mul_precise((row >= col).astype(F32), ld, NT)
    beta_col = bt_ref[0].T
    units = []
    for g in range(heads // 2):
        lanes = slice(g * DK, (g + 1) * DK)
        k_raw = k_ref[:, lanes]
        q_raw = q_ref[:, lanes]
        k_full = k_raw.astype(F32)
        q_full = q_raw.astype(F32)
        k_scale = lax.rsqrt(jnp.sum(k_full * k_full, axis=-1, keepdims=True) + EPSILON)
        q_scale = lax.rsqrt(jnp.sum(q_full * q_full, axis=-1, keepdims=True) + EPSILON) * DK ** (-0.5)
        k_unit = k_full * k_scale
        k_high, k_low = halves(k_unit)
        right = jnp.concatenate([k_high, k_low], axis=1)
        key_key = mul(jnp.concatenate([k_raw, k_raw], axis=1), right, NT) * k_scale
        query_key = mul(jnp.concatenate([q_raw, q_raw], axis=1), right, NT) * q_scale
        units.append((k_unit, q_full * q_scale))
        for h in (2 * g, 2 * g + 1):
            gap = cum_col[:, h:h + 1] - cum_row[h:h + 1, :]
            decay = jnp.where(row >= col, jnp.exp(jnp.minimum(gap, 0.0)), 0.0)
            s_ref[h] = (decay * query_key).astype(BF16)
            system = jnp.where(row > col, decay * key_key, 0.0) * beta_col[:, h:h + 1]
            n_ref[h] = system
            x_ref[h] = jnp.where((row ^ col) == 1, -system, 0.0)
    for level in range(1, 7):
        cross = ((row >> level) ^ (col >> level)) == 1
        left = []
        for h in range(heads):
            part = jnp.where(cross, n_ref[h], 0.0)
            left.append(part + mul(x_ref[h].astype(BF16), part.astype(BF16)))
        for h in range(heads):
            old = x_ref[h]
            x_ref[h] = old - left[h] - mul(left[h].astype(BF16), old.astype(BF16))
    for h in range(heads):
        k_unit, q_unit = units[h // 2]
        cum = cum_col[:, h:h + 1]
        last = cum_row[h:h + 1, TOK - 1:TOK]
        beta = beta_col[:, h:h + 1]
        gamma = jnp.exp(cum)
        value = v_ref[:, h * DK:(h + 1) * DK].astype(F32) * beta
        right = jnp.concatenate([value, k_unit * (beta * gamma)], axis=1)
        write = (right + mul(x_ref[h].astype(BF16), right.astype(BF16))).astype(BF16)
        tail = (jnp.exp(last - cum) * k_unit).astype(BF16)
        moved = mul(write, tail, TN)
        trans = (-moved[DK:]).astype(BF16)
        inject = moved[:DK].astype(BF16)
        read = mul(s_ref[h], write)
        local_ref[h] = read[:, :DK]
        reader_ref[h] = (gamma * q_unit - read[:, DK:]).astype(BF16)
        whole = jnp.exp(jnp.broadcast_to(last, (16, DK)))
        part0 = whole.astype(BF16)
        part1 = (whole - part0.astype(F32)).astype(BF16)
        part2 = (whole - part0.astype(F32) - part1.astype(F32)).astype(BF16)
        line = lax.broadcasted_iota(jnp.int32, (16, DK), 0)
        parts = jnp.where(line == 0, part0.astype(F32), jnp.where(line == 1, part1.astype(F32), part2.astype(F32)))
        parts = jnp.where(line < 3, parts, 0.0).astype(BF16)
        msg_ref[h, 0:128] = trans
        msg_ref[h, 128:256] = inject
        msg_ref[h, 256:272] = parts


def local_terms(query, key, value, log_decay, strength):
    heads = HV // GROUPS
    return pl.pallas_call(
        local_kernel,
        grid=(GROUPS,),
        in_specs=[
            pl.BlockSpec((TOK, heads // 2 * DK), lambda i: (0, i)),
            pl.BlockSpec((TOK, heads // 2 * DK), lambda i: (0, i)),
            pl.BlockSpec((TOK, heads * DK), lambda i: (0, i)),
            pl.BlockSpec((1, heads, TOK), lambda i: (i, 0, 0)),
            pl.BlockSpec((1, heads, TOK), lambda i: (i, 0, 0)),
        ],
        out_specs=[
            pl.BlockSpec((heads, MSG, DK), lambda i: (i, 0, 0)),
            pl.BlockSpec((heads, TOK, DK), lambda i: (i, 0, 0)),
            pl.BlockSpec((heads, TOK, DK), lambda i: (i, 0, 0)),
        ],
        out_shape=[
            jax.ShapeDtypeStruct((HV, MSG, DK), BF16),
            jax.ShapeDtypeStruct((HV, TOK, DK), BF16),
            jax.ShapeDtypeStruct((HV, TOK, DK), F32),
        ],
        scratch_shapes=[
            pltpu.VMEM((heads, TOK, TOK), F32),
            pltpu.VMEM((heads, TOK, TOK), F32),
            pltpu.VMEM((heads, TOK, TOK), BF16),
        ],
        compiler_params=pltpu.CompilerParams(vmem_limit_bytes=VMEM),
        name="local_terms",
    )(query, key, value, log_decay.reshape(GROUPS, heads, TOK), strength.reshape(GROUPS, heads, TOK))


def axis_names():
    seq = lax.axis_index("seq")
    return (lax.div(seq, 8), lax.rem(lax.div(seq, 2), 4), lax.rem(seq, 2), lax.axis_index("batch"))


def device_at(offset):
    z, x, core, y = axis_names()
    dz, dx, dcore, dy = offset
    seq = lax.rem(z + dz, 4) * 8 + lax.rem(x + dx, 4) * 2 + lax.rem(core + dcore, 2)
    return (seq, lax.rem(y + dy, 4))


def greet(offsets):
    barrier = pltpu.get_barrier_semaphore()
    for offset in offsets:
        pl.semaphore_signal(barrier, inc=1, device_id=device_at(offset), device_id_type=MESH)
    pl.semaphore_wait(barrier, len(offsets))


def along(part, d):
    return ((0, 0, 0, d), (0, d, 0, 0), (d, 0, 0, 0))[part]


def across(part, p, q, dcore):
    return ((p, q, dcore, 0), (p, 0, dcore, q), (0, p, dcore, q))[part]


def line_place(part):
    z, x, _, y = axis_names()
    return (y, x, z)[part]


def plane_index(part, offset):
    z, x, core, y = axis_names()
    dz, dx, dcore, dy = offset
    z, x, y = lax.rem(z + dz, 4), lax.rem(x + dx, 4), lax.rem(y + dy, 4)
    first, second = ((z, x), (z, y), (x, y))[part]
    return (first * 4 + second) * 2 + lax.rem(core + dcore, 2)


PAIRS = (
    ((1, 1), (3, 3), (1, 3), (3, 1)),
    ((2, 2),),
    ((1, 0), (3, 0), (0, 1), (0, 3)),
    ((2, 0), (0, 2)),
    ((2, 1), (2, 3)),
    ((1, 2), (3, 2)),
)


def line_copies(sources, targets, semaphores, scatter):
    send, receive, own = semaphores
    copies = []
    for part in range(3):
        place = line_place(part)
        source = sources[part].at[place] if scatter else sources[part]
        copies.append(pltpu.make_async_copy(source, targets[part].at[place], own.at[part]))
    for d in (1, 3, 2):
        for part in range(3):
            place = line_place(part)
            source = sources[part].at[lax.rem(place + d, 4)] if scatter else sources[part]
            copies.append(pltpu.make_async_remote_copy(
                source, targets[part].at[place], send.at[part, d], receive.at[part, d],
                device_id=device_at(along(part, d)), device_id_type=MESH,
            ))
    return copies


def prefix_kernel(map_ref, table_ref, state_ref, tables_ref, inbox, outbox, send, receive, send_back, receive_back, *lines):
    seq, batch = lax.axis_index("seq"), lax.axis_index("batch")
    z, x, core = seq // 8, seq // 2 % 4, seq % 2
    count = inbox.shape[0]
    head = z * 4 + x

    barrier = pltpu.get_barrier_semaphore()
    for other in range(1, count):
        pl.semaphore_signal(
            barrier, inc=1, device_id=(lax.rem(seq + other, count), batch), device_id_type=MESH
        )
    for d in (1, 2, 3):
        pl.semaphore_signal(barrier, inc=1, device_id=device_at((0, 0, 0, d)), device_id_type=MESH)
    pl.semaphore_wait(barrier, count + 2)
    tables = line_copies((table_ref,) * 3, [tables_ref.at[part] for part in range(3)], lines, False)
    for copy in tables:
        copy.start()

    def to_owner(p, q):
        chip = lax.rem(z + p, 4) * 4 + lax.rem(x + q, 4)
        return pltpu.make_async_remote_copy(
            map_ref.at[chip], inbox.at[seq], send.at[p * 4 + q], receive.at[seq],
            device_id=(chip * 2, batch), device_id_type=MESH,
        )

    def own():
        return pltpu.make_async_copy(map_ref.at[head], inbox.at[seq], receive.at[seq])

    def back(place):
        return pltpu.make_async_remote_copy(
            outbox.at[place], state_ref.at[head], send_back.at[place], receive_back.at[head],
            device_id=(place, batch), device_id_type=MESH,
        )

    def own_back():
        return pltpu.make_async_copy(outbox.at[seq], state_ref.at[head], receive_back.at[head])

    far = [offset for group in PAIRS for offset in group]
    for p, q in far:
        to_owner(p, q).start()

    @pl.when(core == 1)
    def _():
        to_owner(0, 0).start()

    @pl.when(core == 0)
    def _():
        own().start()

        def step(place, state):
            pltpu.make_async_copy(inbox.at[place], inbox.at[place], receive.at[place]).wait()
            high, low = halves(state)
            outbox[place] = high

            @pl.when(place == seq)
            def _():
                own_back().start()

            @pl.when(place != seq)
            def _():
                back(place).start()

            both = mul(jnp.concatenate([high, low], axis=0), inbox[place, 0:128])
            parts = inbox[place, 256:272].astype(F32)
            gamma = parts[0:1] + parts[1:2] + parts[2:3]
            return state * gamma + (both[:DK] + both[DK:]) + inbox[place, 128:256].astype(F32)

        lax.fori_loop(0, count, step, jnp.zeros((DK, DK), F32))

        def sent(place, carry):
            @pl.when(place != seq)
            def _():
                back(place).wait_send()

            return carry

        lax.fori_loop(0, count, sent, 0)

    for p, q in far:
        to_owner(p, q).wait_send()

    @pl.when(core == 1)
    def _():
        to_owner(0, 0).wait_send()

    def arrived(place, carry):
        pltpu.make_async_copy(state_ref.at[place], state_ref.at[place], receive_back.at[place]).wait()
        return carry

    lax.fori_loop(0, HV, arrived, 0)
    for copy in tables:
        copy.wait()


def prefix(maps, table, count):
    dma = pltpu.SemaphoreType.DMA
    return pl.pallas_call(
        prefix_kernel,
        out_shape=[
            jax.ShapeDtypeStruct((HV, DK, DK), BF16),
            jax.ShapeDtypeStruct((3, 4) + table.shape, BF16),
        ],
        in_specs=[pl.BlockSpec(memory_space=pltpu.VMEM)] * 2,
        out_specs=[pl.BlockSpec(memory_space=pltpu.VMEM)] * 2,
        scratch_shapes=[
            pltpu.VMEM((count, MSG, DK), BF16),
            pltpu.VMEM((count, DK, DK), BF16),
            dma((HV,)),
            dma((count,)),
            dma((count,)),
            dma((HV,)),
            dma((3, 4)),
            dma((3, 4)),
            dma((3,)),
        ],
        compiler_params=pltpu.CompilerParams(
            collective_id=0, has_side_effects=True, vmem_limit_bytes=VMEM
        ),
        name="prefix",
    )(maps, table)


def finish_kernel(state_ref, reader_ref, local_ref, gate_ref, gain_ref, weight_ref, resid_ref, post_ref, mid_ref, a_ref, b_ref, c_ref, normed_ref):
    step = pl.program_id(0)
    width = weight_ref.shape[1]

    @pl.when(step == 0)
    def _():
        for h in range(HV):
            kept = mul(reader_ref[h], state_ref[h], NT) + local_ref[h]
            scaled = kept * lax.rsqrt(jnp.mean(kept * kept, axis=-1, keepdims=True) + EPSILON)
            gate = gate_ref[:, h * DK:(h + 1) * DK].astype(F32)
            normed_ref[:, h * DK:(h + 1) * DK] = (
                scaled * gain_ref[...] * (gate / (1.0 + jnp.exp(-gate)))
            ).astype(BF16)

    lanes = pl.ds(pl.multiple_of(step * width, width), width)
    mid_ref[:, lanes] = resid_ref[:, lanes].astype(F32) + mul(normed_ref[...], weight_ref[...])

    @pl.when(step == pl.num_programs(0) - 1)
    def _():
        mid = mid_ref[...]
        moe_in = (
            mid * lax.rsqrt(jnp.mean(mid * mid, axis=-1, keepdims=True) + EPSILON) * post_ref[...]
        ).astype(BF16)
        for ref, (low, high) in zip((a_ref, b_ref, c_ref), PARTS):
            ref[...] = moe_in[:, low:high]


def finish(state, reader, local, gate, gain, weight, resid, post):
    depth, width = weight.shape
    tile = 512
    whole2 = lambda i: (0, 0)
    whole3 = lambda i: (0, 0, 0)
    return pl.pallas_call(
        finish_kernel,
        grid=(width // tile,),
        in_specs=[
            pl.BlockSpec((HV, DK, DK), whole3),
            pl.BlockSpec((HV, TOK, DK), whole3),
            pl.BlockSpec((HV, TOK, DK), whole3),
            pl.BlockSpec((TOK, HV * DK), whole2),
            pl.BlockSpec((1, DK), whole2),
            pl.BlockSpec((depth, tile), lambda i: (0, i)),
            pl.BlockSpec((TOK, width), whole2),
            pl.BlockSpec((1, width), whole2),
        ],
        out_specs=[pl.BlockSpec((TOK, width), whole2)]
        + [pl.BlockSpec((TOK, high - low), whole2) for low, high in PARTS],
        out_shape=[jax.ShapeDtypeStruct((TOK, width), F32)]
        + [jax.ShapeDtypeStruct((TOK, high - low), BF16) for low, high in PARTS],
        scratch_shapes=[pltpu.VMEM((TOK, HV * DK), BF16)],
        compiler_params=pltpu.CompilerParams(vmem_limit_bytes=VMEM),
        name="finish",
    )(state, reader, local, gate, gain[None], weight, resid, post[None])


ORDER = [(p, q, dcore) for group in PAIRS for dcore in (0, 1) for p, q in group] + [(0, 0, 1), (0, 0, 0)]


def plane_copy(source, target, send, receive, part, step):
    p, q, dcore = step
    offset = across(part, p, q, dcore)
    slot = p * 8 + q * 2 + dcore
    if step == (0, 0, 0):
        return pltpu.make_async_copy(source, target, receive.at[part, slot])
    return pltpu.make_async_remote_copy(
        source, target, send.at[part, slot], receive.at[part, slot],
        device_id=device_at(offset), device_id_type=MESH,
    )


def wait_sent(copy, step):
    if step != (0, 0, 0):
        copy.wait_send()


def wait_arrived(copy, step):
    if step == (0, 0, 0):
        copy.wait()
    else:
        copy.wait_recv()


def plane_offsets():
    return sorted(set(across(part, *step) for part in range(3) for step in ORDER) - {(0, 0, 0, 0)})


def picked(slot):
    rows = lax.broadcasted_iota(jnp.int32, (ROWS, TOK), 0).astype(F32)
    return slot[..., None, :] == rows


def whole_copies(sources, targets, semaphores):
    return [pltpu.make_async_copy(sources[part], targets[part], semaphores.at[part]) for part in range(3)]


def expert_rows(step, buffers, x_ref):
    a_ref, b_ref, c_ref = buffers
    wa, wb = a_ref.shape[2], b_ref.shape[2]
    pair, core = step // 2, step % 2
    tile = pl.ds(pl.multiple_of(pair * 16, 16), 16)
    parts_c = [[c_ref[(x * 4 + y) * 2 + core, tile].astype(F32) for y in range(4)] for x in range(4)]
    for n in range(2):
        z = pair * 2 + n
        parts_b = [b_ref[(z * 4 + y) * 2 + core].astype(F32) for y in range(4)]
        for x in range(4):
            rows = slice((n * 4 + x) * 32, (n * 4 + x) * 32 + 32)
            x_ref[rows, 0:wa] = a_ref[(z * 4 + x) * 2 + core]
            x_ref[rows, wa:wa + wb] = jnp.concatenate(
                [parts_b[y][x * ROWS:(x + 1) * ROWS] for y in range(4)], axis=0
            ).astype(BF16)
            x_ref[rows, wa + wb:] = jnp.concatenate(
                [parts_c[x][y][n * ROWS:(n + 1) * ROWS] for y in range(4)], axis=0
            ).astype(BF16)


def expert_results(step, result, stages):
    a_ref, b_ref, c_ref = stages
    wa, wb = a_ref.shape[2], b_ref.shape[2]
    pair, core = step // 2, step % 2
    tile = pl.ds(pl.multiple_of(pair * 16, 16), 16)

    def piece(n, x, y, low, high):
        start = ((n * 4 + x) * 4 + y) * ROWS
        return result[start:start + ROWS, low:high]

    for n in range(2):
        z = pair * 2 + n
        for x in range(4):
            start = (n * 4 + x) * 32
            a_ref[(z * 4 + x) * 2 + core] = result[start:start + 32, 0:wa].astype(BF16)
        for y in range(4):
            b_ref[(z * 4 + y) * 2 + core] = jnp.concatenate(
                [piece(n, x, y, wa, wa + wb) for x in range(4)], axis=0
            ).astype(BF16)
    for x in range(4):
        for y in range(4):
            c_ref[(x * 4 + y) * 2 + core, tile] = jnp.concatenate(
                [piece(n, x, y, wa + wb, result.shape[1]) for n in range(2)], axis=0
            ).astype(BF16)


def moe_kernel(*refs):
    slot_ref, share_ref, mid_ref, rows, up_ref, down_ref = refs[0], refs[1], refs[2], refs[3:6], refs[6], refs[7]
    out_ref, arrived, returned = refs[8], refs[9:12], refs[12:15]
    lines, stages, buffers, sums, totals = refs[15:18], refs[18:21], refs[21:24], refs[24:27], refs[27:30]
    up_v, down_v, x_ref = refs[30:33]
    gather_semaphores, scatter_semaphores = refs[33:36], refs[36:39]
    send, receive, send_back, receive_back, load, fetch = refs[39:45]
    hidden_width = down_ref.shape[1]

    def weight_copies(j):
        return (
            pltpu.make_async_copy(up_ref.at[j], up_v, fetch.at[0]),
            pltpu.make_async_copy(down_ref.at[j], down_v, fetch.at[1]),
        )

    weights = weight_copies(0)
    for copy in weights:
        copy.start()
    greet(plane_offsets())
    gathers = line_copies(rows, lines, gather_semaphores, False)
    for copy in gathers:
        copy.start()
    for copy in gathers:
        copy.wait()

    out_copies = []
    for j in range(2):
        copies = []
        for g in range(2):
            steps = ORDER[16 * g:16 * g + 16]
            for part in range(3):
                places = [plane_index(part, across(part, *step)) for step in steps]

                def fill(pair, carry, part=part, places=places, g=g, j=j):
                    packed = []
                    for n in range(2):
                        a = pair * 2 + n
                        slots = jnp.concatenate([slot_ref[part, place, a, j:j + 1] for place in places], axis=0)
                        take = jnp.where(picked(slots), 1.0, 0.0).reshape(16 * ROWS, TOK).astype(BF16)
                        packed.append(mul(take, lines[part][a]).reshape(16, ROWS, lines[part].shape[2]))
                    tile = pl.ds(pl.multiple_of(pair * 16, 16), 16)
                    stages[part][j, 16 * g:16 * g + 16, tile] = jnp.concatenate(packed, axis=1).astype(BF16)
                    return carry

                lax.fori_loop(0, 2, fill, 0)
                here = plane_index(part, (0, 0, 0, 0))
                for i, step in enumerate(steps):
                    copy = plane_copy(
                        stages[part].at[j, 16 * g + i], arrived[part].at[j, here],
                        send.at[j], receive.at[j], part, step,
                    )
                    copy.start()
                    copies.append((copy, step))
        out_copies.append(copies)

    back_copies = []
    for j in range(2):
        for copy, step in out_copies[j]:
            wait_arrived(copy, step)
        loads = whole_copies([ref.at[j] for ref in arrived], buffers, load)
        for copy in loads:
            copy.start()
        for copy, step in out_copies[j]:
            wait_sent(copy, step)
        for copy in weights:
            copy.wait()
        for copy in loads:
            copy.wait()

        def expert_step(step, carry, j=j):
            expert_rows(step, buffers, x_ref)
            both = mul(x_ref[...], up_v[...])
            gate = both[:, :hidden_width]
            hidden = (gate / (1.0 + jnp.exp(-gate)) * both[:, hidden_width:]).astype(BF16)
            expert_results(step, mul(hidden, down_v[...]), [ref.at[j] for ref in stages])
            return carry

        lax.fori_loop(0, 4, expert_step, 0)
        if j == 0:
            weights = weight_copies(1)
            for copy in weights:
                copy.start()
        copies = []
        for step in ORDER:
            for part in range(3):
                copy = plane_copy(
                    stages[part].at[j, plane_index(part, across(part, *step))],
                    returned[part].at[j, plane_index(part, (0, 0, 0, 0))],
                    send_back.at[j], receive_back.at[j], part, step,
                )
                copy.start()
                copies.append((copy, step))
        back_copies.append(copies)

    scatters = line_copies(lines, sums, scatter_semaphores, True)
    own, others = scatters[0:3], scatters[3:]
    row = lax.broadcasted_iota(jnp.int32, (2 * ROWS, TOK), 0).astype(F32)
    for j in range(2):
        for copy, step in back_copies[j]:
            wait_arrived(copy, step)
        loads = whole_copies([ref.at[j] for ref in returned], buffers, load)
        for copy in loads:
            copy.start()
        for part in range(3):
            loads[part].wait()
            width = buffers[part].shape[2]
            for n, d in enumerate((1, 3, 2, 0)):
                a = lax.rem(line_place(part) + d, 4)
                tile = pl.ds(pl.multiple_of(a // 2 * 16, 16), 16)
                shift = (a % 2 * ROWS).astype(F32)
                slots = slot_ref[part, :, a, j] + shift
                give = jnp.where(slots[:, None, :] == row, share_ref[part, :, a, j][:, None, :], 0.0)
                high, low = halves(give.reshape(64 * ROWS, TOK))
                values = buffers[part][:, tile].reshape(64 * ROWS, width)
                both = mul(jnp.concatenate([high, low], axis=1), values, TN)
                if j == 0:
                    totals[part][a] = both[:TOK] + both[TOK:]
                else:
                    lines[part][a] = (totals[part][a] + both[:TOK] + both[TOK:]).astype(BF16)
                    copy = own[part] if d == 0 else others[3 * n + part]
                    copy.start()
    for part, (low, high) in enumerate(PARTS):
        for n in range(3):
            others[3 * n + part].wait()
        own[part].wait()
        total = mid_ref[:, low:high]
        for a in range(4):
            total = total + sums[part][a].astype(F32)
        out_ref[:, low:high] = total.astype(BF16)
    for copies in back_copies:
        for copy, step in copies:
            wait_sent(copy, step)


def moe(slots, shares, mid, rows, up, down):
    dma = pltpu.SemaphoreType.DMA
    widths = [part.shape[1] for part in rows]
    exchange = [jax.ShapeDtypeStruct((2, 32, 4 * ROWS, width), BF16) for width in widths]
    return pl.pallas_call(
        moe_kernel,
        in_specs=[pl.BlockSpec(memory_space=pltpu.VMEM)] * 6 + [pl.BlockSpec(memory_space=pl.ANY)] * 2,
        out_specs=[pl.BlockSpec(memory_space=pltpu.VMEM)] + [pl.BlockSpec(memory_space=pl.ANY)] * 6,
        out_shape=[jax.ShapeDtypeStruct(mid.shape, BF16)] + exchange + exchange,
        scratch_shapes=[pltpu.VMEM((4, TOK, width), BF16) for width in widths]
        + [pltpu.VMEM((2, 32, 4 * ROWS, width), BF16) for width in widths]
        + [pltpu.VMEM((32, 4 * ROWS, width), BF16) for width in widths]
        + [pltpu.VMEM((4, TOK, width), BF16) for width in widths]
        + [pltpu.VMEM((4, TOK, width), F32) for width in widths]
        + [pltpu.VMEM(up.shape[1:], BF16), pltpu.VMEM(down.shape[1:], BF16), pltpu.VMEM((256, up.shape[1]), BF16)]
        + [dma((3, 4)), dma((3, 4)), dma((3,))] * 2
        + [dma((2, 3, 32))] * 4
        + [dma((3,)), dma((2,))],
        compiler_params=pltpu.CompilerParams(
            collective_id=1, has_side_effects=True, vmem_limit_bytes=VMEM
        ),
        name="moe",
    )(slots, shares, mid, *rows, up, down)[0]


def routing_table(ids, weights):
    high, low = halves(weights)
    return jnp.concatenate([ids.T.astype(BF16), high.T, low.T, jnp.zeros((2, TOK), BF16)], axis=0)


def routes(tables, top, exp_dev):
    z, x, core, y = axis_names()
    place = jnp.arange(32, dtype=jnp.int32)
    first, second, side = place // 8, place // 2 % 4, place % 2
    device = jnp.stack([
        place * 4 + y,
        (first * 8 + x * 2 + side) * 4 + second,
        (z * 8 + first * 2 + side) * 4 + second,
    ])
    numbers = tables[:, :, 0:top].astype(F32)
    share = tables[:, :, top:2 * top].astype(F32) + tables[:, :, 2 * top:3 * top].astype(F32)
    expert = (device[:, :, None] * exp_dev + jnp.arange(exp_dev)).astype(F32)
    named = numbers[:, None, :, None] == expert[:, :, None, :, None, None]
    chosen = jnp.sum(named.astype(F32), axis=4)
    given = jnp.sum(jnp.where(named, share[:, None, :, None], 0.0), axis=4)
    earlier = jnp.triu(jnp.ones((TOK, TOK), BF16), 1)
    rank = mul(chosen.astype(BF16).reshape(-1, TOK), earlier).reshape(chosen.shape)
    return jnp.where(chosen > 0, rank, -1.0), given


def shards(
    query_rows,
    key_rows,
    value_rows,
    gate_z,
    log_decay,
    write_strength,
    norm_gain,
    out_weight,
    residual,
    post_gain,
    expert_ids,
    gate_scores,
    expert_up,
    expert_down,
):
    exp_dev = expert_up.shape[0]
    scores = gate_scores[0]
    weights = scores / jnp.sum(scores, axis=-1, keepdims=True)
    table = routing_table(expert_ids[0], weights)
    maps, reader, local = local_terms(
        query_rows[0], key_rows[0], value_rows[0], log_decay[0], write_strength[0]
    )
    states, tables = prefix(maps, table, lax.axis_size("seq"))
    mid, *rows = finish(
        states, reader, local, gate_z[0], norm_gain, out_weight, residual[0], post_gain
    )
    slots, shares = routes(tables, expert_ids.shape[2], exp_dev)
    return moe(slots, shares, mid, rows, expert_up, expert_down)[None]


def solution(mesh):
    return jax.shard_map(
        shards,
        mesh=mesh,
        in_specs=(
            P("batch", "seq", None),
            P("batch", "seq", None),
            P("batch", "seq", None),
            P("batch", "seq", None),
            P("batch", None, "seq"),
            P("batch", None, "seq"),
            P(),
            P(),
            P("batch", "seq", None),
            P(),
            P("batch", "seq", None),
            P("batch", "seq", None),
            P(("seq", "batch"), None, None),
            P(("seq", "batch"), None, None),
        ),
        out_specs=P("batch", "seq", None),
        check_vma=False,
    )
```

```python
import functools

import jax
import jax.numpy as jnp
from jax import lax
from jax.experimental import pallas as pl
from jax.experimental.pallas import tpu as pltpu
from jax.sharding import PartitionSpec as P

TOK = 128
DK = 128
HV = 16
HK = 8
GROUPS = 2
ROWS = 8
MSG = 272
VMEM = 60 << 20
PARTS = ((0, 768), (768, 1408), (1408, 2048))
MESH = pl.DeviceIdType.MESH
EPSILON = 1e-06
PRECISE = lax.Precision.HIGHEST
F32 = jnp.float32
BF16 = jnp.bfloat16

NN = (((1,), (0,)), ((), ()))
NT = (((1,), (1,)), ((), ()))
TN = (((0,), (0,)), ((), ()))


def mul(a, b, dims=NN):
    return lax.dot_general(a, b, dims, preferred_element_type=F32)


def mul_precise(a, b, dims=NN):
    return lax.dot_general(a, b, dims, preferred_element_type=F32, precision=PRECISE)


def halves(a):
    high = a.astype(BF16)
    return high, (a - high.astype(F32)).astype(BF16)


def axis_names():
    seq = lax.axis_index("seq")
    return (lax.div(seq, 8), lax.rem(lax.div(seq, 2), 4), lax.rem(seq, 2), lax.axis_index("batch"))


def device_at(offset):
    z, x, core, y = axis_names()
    dz, dx, dcore, dy = offset
    seq = lax.rem(z + dz, 4) * 8 + lax.rem(x + dx, 4) * 2 + lax.rem(core + dcore, 2)
    return (seq, lax.rem(y + dy, 4))


def greet(offsets):
    barrier = pltpu.get_barrier_semaphore()
    for offset in offsets:
        pl.semaphore_signal(barrier, inc=1, device_id=device_at(offset), device_id_type=MESH)
    pl.semaphore_wait(barrier, len(offsets))


def along(part, d):
    return ((0, 0, 0, d), (0, d, 0, 0), (d, 0, 0, 0))[part]


def across(part, p, q, dcore):
    return ((p, q, dcore, 0), (p, 0, dcore, q), (0, p, dcore, q))[part]


def line_place(part):
    z, x, _, y = axis_names()
    return (y, x, z)[part]


def plane_index(part, offset):
    z, x, core, y = axis_names()
    dz, dx, dcore, dy = offset
    z, x, y = lax.rem(z + dz, 4), lax.rem(x + dx, 4), lax.rem(y + dy, 4)
    first, second = ((z, x), (z, y), (x, y))[part]
    return (first * 4 + second) * 2 + lax.rem(core + dcore, 2)


PAIRS = (
    ((1, 1), (3, 3), (1, 3), (3, 1)),
    ((2, 2),),
    ((1, 0), (3, 0), (0, 1), (0, 3)),
    ((2, 0), (0, 2)),
    ((2, 1), (2, 3)),
    ((1, 2), (3, 2)),
)


def line_copies(sources, targets, semaphores, scatter):
    send, receive, own = semaphores
    copies = []
    for part in range(3):
        place = line_place(part)
        source = sources[part].at[place] if scatter else sources[part]
        copies.append(pltpu.make_async_copy(source, targets[part].at[place], own.at[part]))
    for d in (1, 3, 2):
        for part in range(3):
            place = line_place(part)
            source = sources[part].at[lax.rem(place + d, 4)] if scatter else sources[part]
            copies.append(pltpu.make_async_remote_copy(
                source, targets[part].at[place], send.at[part, d], receive.at[part, d],
                device_id=device_at(along(part, d)), device_id_type=MESH,
            ))
    return copies


def local_terms(g, q_ref, k_ref, v_ref, ld_ref, bt_ref, map_ref, reader_ref, local_ref, n_ref, x_ref, s_ref):
    heads = HV // GROUPS
    row = lax.broadcasted_iota(jnp.int32, (TOK, TOK), 0)
    col = lax.broadcasted_iota(jnp.int32, (TOK, TOK), 1)
    ld = ld_ref[g]
    cum_row = mul_precise(ld, (row <= col).astype(F32))
    cum_col = mul_precise((row >= col).astype(F32), ld, NT)
    beta_col = bt_ref[g].T
    units = []
    for pair in range(heads // 2):
        key_head = g * (heads // 2) + pair
        lanes = slice(key_head * DK, (key_head + 1) * DK)
        k_raw = k_ref[:, lanes]
        q_raw = q_ref[:, lanes]
        k_full = k_raw.astype(F32)
        q_full = q_raw.astype(F32)
        k_scale = lax.rsqrt(jnp.sum(k_full * k_full, axis=-1, keepdims=True) + EPSILON)
        q_scale = lax.rsqrt(jnp.sum(q_full * q_full, axis=-1, keepdims=True) + EPSILON) * DK ** (-0.5)
        k_unit = k_full * k_scale
        k_high, k_low = halves(k_unit)
        right = jnp.concatenate([k_high, k_low], axis=1)
        key_key = mul(jnp.concatenate([k_raw, k_raw], axis=1), right, NT) * k_scale
        query_key = mul(jnp.concatenate([q_raw, q_raw], axis=1), right, NT) * q_scale
        units.append((k_unit, q_full * q_scale))
        for h in (2 * pair, 2 * pair + 1):
            gap = cum_col[:, h:h + 1] - cum_row[h:h + 1, :]
            decay = jnp.where(row >= col, jnp.exp(jnp.minimum(gap, 0.0)), 0.0)
            s_ref[h] = (decay * query_key).astype(BF16)
            system = jnp.where(row > col, decay * key_key, 0.0) * beta_col[:, h:h + 1]
            n_ref[h] = system
            x_ref[h] = jnp.where((row ^ col) == 1, -system, 0.0)
    for level in range(1, 7):
        cross = ((row >> level) ^ (col >> level)) == 1
        left = []
        for h in range(heads):
            part = jnp.where(cross, n_ref[h], 0.0)
            left.append(part + mul(x_ref[h].astype(BF16), part.astype(BF16)))
        for h in range(heads):
            old = x_ref[h]
            x_ref[h] = old - left[h] - mul(left[h].astype(BF16), old.astype(BF16))
    line = lax.broadcasted_iota(jnp.int32, (16, DK), 0)
    for h in range(heads):
        k_unit, q_unit = units[h // 2]
        cum = cum_col[:, h:h + 1]
        last = cum_row[h:h + 1, TOK - 1:TOK]
        beta = beta_col[:, h:h + 1]
        gamma = jnp.exp(cum)
        head = g * heads + h
        value = v_ref[:, head * DK:(head + 1) * DK].astype(F32) * beta
        right = jnp.concatenate([value, k_unit * (beta * gamma)], axis=1)
        write = (right + mul(x_ref[h].astype(BF16), right.astype(BF16))).astype(BF16)
        tail = (jnp.exp(last - cum) * k_unit).astype(BF16)
        moved = mul(write, tail, TN)
        read = mul(s_ref[h], write)
        local_ref[head] = read[:, :DK]
        reader_ref[head] = (gamma * q_unit - read[:, DK:]).astype(BF16)
        whole = jnp.exp(jnp.broadcast_to(last, (16, DK)))
        part0 = whole.astype(BF16)
        part1 = (whole - part0.astype(F32)).astype(BF16)
        part2 = (whole - part0.astype(F32) - part1.astype(F32)).astype(BF16)
        parts = jnp.where(line == 0, part0.astype(F32), jnp.where(line == 1, part1.astype(F32), part2.astype(F32)))
        map_ref[head, 0:128] = (-moved[DK:]).astype(BF16)
        map_ref[head, 128:256] = moved[:DK].astype(BF16)
        map_ref[head, 256:272] = jnp.where(line < 3, parts, 0.0).astype(BF16)


def mixer_kernel(
    q_ref, k_ref, v_ref, ld_ref, bt_ref, gate_ref, gain_ref, resid_ref, post_ref, ids_hbm, scores_hbm, weight_ref,
    mid_ref, a_ref, b_ref, c_ref, tables_ref,
    map_ref, reader_ref, local_ref, n_ref, x_ref, s_ref, weight_v, normed_ref, state_ref, inbox, outbox, table_ref, ids_ref, scores_ref,
    send, receive, send_back, receive_back, fetch, *lines,
):
    seq, batch = lax.axis_index("seq"), lax.axis_index("batch")
    z, x, core = seq // 8, seq // 2 % 4, seq % 2
    count = inbox.shape[0]
    heads = HV // GROUPS
    owned = (z + x) % 2 * heads + z * 2 + x // 2

    weights = pltpu.make_async_copy(weight_ref, weight_v, fetch.at[0])
    routing = (
        pltpu.make_async_copy(ids_hbm, ids_ref, fetch.at[1]),
        pltpu.make_async_copy(scores_hbm, scores_ref, fetch.at[2]),
    )
    for copy in routing:
        copy.start()
    weights.start()
    barrier = pltpu.get_barrier_semaphore()
    for other in range(1, count):
        pl.semaphore_signal(
            barrier, inc=1, device_id=(lax.rem(seq + other, count), batch), device_id_type=MESH
        )
    for d in (1, 2, 3):
        pl.semaphore_signal(barrier, inc=1, device_id=device_at((0, 0, 0, d)), device_id_type=MESH)

    def to_owner(g, n):
        i = lax.rem(n + z * 4 + x, heads)
        head = g * heads + i
        to_z = i // 2
        owner = (to_z * 4 + i % 2 * 2 + (to_z + g) % 2) * 2
        remote = pltpu.make_async_remote_copy(
            map_ref.at[head], inbox.at[seq], send.at[head], receive.at[seq],
            device_id=(owner, batch), device_id_type=MESH,
        )
        own = pltpu.make_async_copy(map_ref.at[head], inbox.at[seq], receive.at[seq])
        return owner, remote, own

    def ship(g):
        for n in range(heads):
            owner, remote, own = to_owner(g, n)

            @pl.when(owner == seq)
            def _():
                own.start()

            @pl.when(owner != seq)
            def _():
                remote.start()

    local_args = (q_ref, k_ref, v_ref, ld_ref, bt_ref, map_ref, reader_ref, local_ref, n_ref, x_ref, s_ref)
    local_terms(0, *local_args)
    pl.semaphore_wait(barrier, count + 2)
    ship(0)
    for copy in routing:
        copy.wait()
    top = ids_ref.shape[0]
    numbers = jnp.concatenate([ids_ref[k] for k in range(top)], axis=0).astype(F32)
    scores = jnp.concatenate([scores_ref[k] for k in range(top)], axis=0)
    high, low = halves(scores / jnp.sum(scores, axis=0, keepdims=True))
    spare = jnp.zeros((16 - numbers.shape[0], TOK), F32)
    for n, value in enumerate((numbers, high.astype(F32), low.astype(F32))):
        table_ref[16 * n:16 * n + 16] = jnp.concatenate([value, spare], axis=0).astype(BF16)
    tables = line_copies((table_ref,) * 3, [tables_ref.at[part] for part in range(3)], lines, False)
    for copy in tables:
        copy.start()
    local_terms(1, *local_args)
    ship(1)

    def back(place):
        return pltpu.make_async_remote_copy(
            outbox.at[place], state_ref.at[owned], send_back.at[place], receive_back.at[owned],
            device_id=(place, batch), device_id_type=MESH,
        )

    @pl.when(core == 0)
    def _():
        def step(place, state):
            pltpu.make_async_copy(inbox.at[place], inbox.at[place], receive.at[place]).wait()
            high, low = halves(state)
            outbox[place] = high

            @pl.when(place == seq)
            def _():
                pltpu.make_async_copy(outbox.at[seq], state_ref.at[owned], receive_back.at[owned]).start()

            @pl.when(place != seq)
            def _():
                back(place).start()

            both = mul(jnp.concatenate([high, low], axis=0), inbox[place, 0:128])
            parts = inbox[place, 256:272].astype(F32)
            gamma = parts[0:1] + parts[1:2] + parts[2:3]
            return state * gamma + (both[:DK] + both[DK:]) + inbox[place, 128:256].astype(F32)

        lax.fori_loop(0, count, step, jnp.zeros((DK, DK), F32))

    for h in range(HV):
        pltpu.make_async_copy(state_ref.at[h], state_ref.at[h], receive_back.at[h]).wait()
        kept = mul(reader_ref[h], state_ref[h], NT) + local_ref[h]
        scaled = kept * lax.rsqrt(jnp.mean(kept * kept, axis=-1, keepdims=True) + EPSILON)
        gate = gate_ref[:, h * DK:(h + 1) * DK].astype(F32)
        normed_ref[:, h * DK:(h + 1) * DK] = (
            scaled * gain_ref[...] * (gate / (1.0 + jnp.exp(-gate)))
        ).astype(BF16)
    weights.wait()
    width = mid_ref.shape[1]
    tile = 512
    total = jnp.zeros((TOK, 1), F32)
    for start in range(0, width, tile):
        lanes = slice(start, start + tile)
        mid = resid_ref[:, lanes].astype(F32) + mul(normed_ref[...], weight_v[:, lanes])
        mid_ref[:, lanes] = mid
        total = total + jnp.sum(mid * mid, axis=-1, keepdims=True)
    scale = lax.rsqrt(total / width + EPSILON)
    for ref, (low, high) in zip((a_ref, b_ref, c_ref), PARTS):
        ref[...] = (mid_ref[:, low:high] * scale * post_ref[:, low:high]).astype(BF16)

    for g in range(GROUPS):
        for n in range(heads):
            owner, remote, _ = to_owner(g, n)

            @pl.when(owner != seq)
            def _():
                remote.wait_send()

    @pl.when(core == 0)
    def _():
        def sent(place, carry):
            @pl.when(place != seq)
            def _():
                back(place).wait_send()

            return carry

        lax.fori_loop(0, count, sent, 0)

    for copy in tables:
        copy.wait()


def mixer(query, key, value, log_decay, strength, gate, gain, resid, post, ids, scores, weight, count):
    heads = HV // GROUPS
    width = weight.shape[1]
    dma = pltpu.SemaphoreType.DMA
    vmem = pltpu.VMEM
    return pl.pallas_call(
        mixer_kernel,
        in_specs=[pl.BlockSpec(memory_space=vmem)] * 9 + [pl.BlockSpec(memory_space=pl.ANY)] * 3,
        out_specs=[pl.BlockSpec(memory_space=vmem)] * 5,
        out_shape=[jax.ShapeDtypeStruct((TOK, width), F32)]
        + [jax.ShapeDtypeStruct((TOK, high - low), BF16) for low, high in PARTS]
        + [jax.ShapeDtypeStruct((3, 4, 48, TOK), BF16)],
        scratch_shapes=[
            vmem((HV, MSG, DK), BF16),
            vmem((HV, TOK, DK), BF16),
            vmem((HV, TOK, DK), F32),
            vmem((heads, TOK, TOK), F32),
            vmem((heads, TOK, TOK), F32),
            vmem((heads, TOK, TOK), BF16),
            vmem(weight.shape, BF16),
            vmem((TOK, weight.shape[0]), BF16),
            vmem((HV, DK, DK), BF16),
            vmem((count, MSG, DK), BF16),
            vmem((count, DK, DK), BF16),
            vmem((48, TOK), BF16),
            vmem(ids.shape, jnp.int32),
            vmem(scores.shape, F32),
            dma((HV,)),
            dma((count,)),
            dma((count,)),
            dma((HV,)),
            dma((3,)),
            dma((3, 4)),
            dma((3, 4)),
            dma((3,)),
        ],
        compiler_params=pltpu.CompilerParams(
            collective_id=0, has_side_effects=True, vmem_limit_bytes=VMEM
        ),
        name="mixer",
    )(
        query, key, value, log_decay.reshape(GROUPS, heads, TOK), strength.reshape(GROUPS, heads, TOK),
        gate, gain[None], resid, post[None], ids, scores, weight,
    )


ORDER = [(p, q, dcore) for group in PAIRS for dcore in (0, 1) for p, q in group] + [(0, 0, 1), (0, 0, 0)]


def plane_copy(source, target, send, receive, part, step):
    p, q, dcore = step
    offset = across(part, p, q, dcore)
    slot = p * 8 + q * 2 + dcore
    if step == (0, 0, 0):
        return pltpu.make_async_copy(source, target, receive.at[part, slot])
    return pltpu.make_async_remote_copy(
        source, target, send.at[part, slot], receive.at[part, slot],
        device_id=device_at(offset), device_id_type=MESH,
    )


def wait_sent(copy, step):
    if step != (0, 0, 0):
        copy.wait_send()


def wait_arrived(copy, step):
    if step == (0, 0, 0):
        copy.wait()
    else:
        copy.wait_recv()


def plane_offsets():
    return sorted(set(across(part, *step) for part in range(3) for step in ORDER) - {(0, 0, 0, 0)})


def picked(slot):
    rows = lax.broadcasted_iota(jnp.int32, (ROWS, TOK), 0).astype(F32)
    return slot[..., None, :] == rows


def whole_copies(sources, targets, semaphores):
    return [pltpu.make_async_copy(sources[part], targets[part], semaphores.at[part]) for part in range(3)]


def expert_rows(step, buffers, x_ref):
    a_ref, b_ref, c_ref = buffers
    wa, wb = a_ref.shape[2], b_ref.shape[2]
    pair, core = step // 2, step % 2
    tile = pl.ds(pl.multiple_of(pair * 16, 16), 16)
    parts_c = [[c_ref[(x * 4 + y) * 2 + core, tile].astype(F32) for y in range(4)] for x in range(4)]
    for n in range(2):
        z = pair * 2 + n
        parts_b = [b_ref[(z * 4 + y) * 2 + core].astype(F32) for y in range(4)]
        for x in range(4):
            rows = slice((n * 4 + x) * 32, (n * 4 + x) * 32 + 32)
            x_ref[rows, 0:wa] = a_ref[(z * 4 + x) * 2 + core]
            x_ref[rows, wa:wa + wb] = jnp.concatenate(
                [parts_b[y][x * ROWS:(x + 1) * ROWS] for y in range(4)], axis=0
            ).astype(BF16)
            x_ref[rows, wa + wb:] = jnp.concatenate(
                [parts_c[x][y][n * ROWS:(n + 1) * ROWS] for y in range(4)], axis=0
            ).astype(BF16)


def expert_results(step, result, stages):
    a_ref, b_ref, c_ref = stages
    wa, wb = a_ref.shape[2], b_ref.shape[2]
    pair, core = step // 2, step % 2
    tile = pl.ds(pl.multiple_of(pair * 16, 16), 16)

    def piece(n, x, y, low, high):
        start = ((n * 4 + x) * 4 + y) * ROWS
        return result[start:start + ROWS, low:high]

    for n in range(2):
        z = pair * 2 + n
        for x in range(4):
            start = (n * 4 + x) * 32
            a_ref[(z * 4 + x) * 2 + core] = result[start:start + 32, 0:wa].astype(BF16)
        for y in range(4):
            b_ref[(z * 4 + y) * 2 + core] = jnp.concatenate(
                [piece(n, x, y, wa, wa + wb) for x in range(4)], axis=0
            ).astype(BF16)
    for x in range(4):
        for y in range(4):
            c_ref[(x * 4 + y) * 2 + core, tile] = jnp.concatenate(
                [piece(n, x, y, wa + wb, result.shape[1]) for n in range(2)], axis=0
            ).astype(BF16)


def fill_slots(tables_ref, slot_ref, share_ref, top):
    z, x, _, y = axis_names()
    line = lax.broadcasted_iota(jnp.int32, (64, TOK), 0)
    half, place = line // 32, line % 32
    first, second, side = place // 8, place // 2 % 4, place % 2
    device = (
        place * 4 + y,
        (first * 8 + x * 2 + side) * 4 + second,
        (z * 8 + first * 2 + side) * 4 + second,
    )
    row = lax.broadcasted_iota(jnp.int32, (TOK, TOK), 0)
    col = lax.broadcasted_iota(jnp.int32, (TOK, TOK), 1)
    earlier = (row < col).astype(F32).astype(BF16)
    for part in range(3):
        expert = (device[part] * 2 + half).astype(F32)
        for a in range(4):
            table = tables_ref[part, a].astype(F32)
            chosen = jnp.zeros((64, TOK), F32)
            given = jnp.zeros((64, TOK), F32)
            for k in range(top):
                named = table[k:k + 1] == expert
                share = table[16 + k:17 + k] + table[32 + k:33 + k]
                chosen = jnp.where(named, 1.0, chosen)
                given = jnp.where(named, share, given)
            rank = mul(chosen.astype(BF16), earlier)
            slot_ref[part, a] = jnp.where(chosen > 0, rank, -1.0)
            share_ref[part, a] = given


def moe_kernel(top, *refs):
    tables_ref, mid_ref, rows, up_ref, down_ref = refs[0], refs[1], refs[2:5], refs[5], refs[6]
    out_ref, arrived, returned, staged = refs[7], refs[8:11], refs[11:14], refs[14:17]
    lines, stages, buffers, sums, totals = refs[17:20], refs[20:23], refs[23:26], refs[26:29], refs[29:32]
    up_v, down_v, x_ref, slot_ref, share_ref = refs[32:37]
    gather_semaphores, scatter_semaphores = refs[37:40], refs[40:43]
    send, receive, send_back, receive_back, load, fetch, store = refs[43:50]
    hidden_width = down_ref.shape[1]

    def weight_copies(j):
        return (
            pltpu.make_async_copy(up_ref.at[j], up_v, fetch.at[0]),
            pltpu.make_async_copy(down_ref.at[j], down_v, fetch.at[1]),
        )

    weights = weight_copies(0)
    for copy in weights:
        copy.start()
    greet(plane_offsets())
    gathers = line_copies(rows, lines, gather_semaphores, False)
    for copy in gathers:
        copy.start()
    fill_slots(tables_ref, slot_ref, share_ref, top)
    for copy in gathers:
        copy.wait()

    out_copies = []
    for j in range(2):
        copies = []
        for g in range(2):
            steps = ORDER[16 * g:16 * g + 16]
            group = slice(16 * g, 16 * g + 16)
            stores = []
            for part in range(3):
                places = [plane_index(part, across(part, *step)) for step in steps]

                def fill(pair, carry, part=part, places=places, group=group, j=j):
                    packed = []
                    for n in range(2):
                        a = pair * 2 + n
                        slots = jnp.concatenate(
                            [slot_ref[part, a, pl.ds(place + 32 * j, 1)] for place in places], axis=0
                        )
                        take = jnp.where(picked(slots), 1.0, 0.0).reshape(16 * ROWS, TOK).astype(BF16)
                        packed.append(mul(take, lines[part][a]).reshape(16, ROWS, lines[part].shape[2]))
                    tile = pl.ds(pl.multiple_of(pair * 16, 16), 16)
                    stages[part][j, group, tile] = jnp.concatenate(packed, axis=1).astype(BF16)
                    return carry

                lax.fori_loop(0, 2, fill, 0)
                stores.append(pltpu.make_async_copy(
                    stages[part].at[j, group], staged[part].at[j, group], store.at[part]
                ))
                stores[part].start()
            for copy in stores:
                copy.wait()
            for i, step in enumerate(steps):
                for part in range(3):
                    here = plane_index(part, (0, 0, 0, 0))
                    copy = plane_copy(
                        staged[part].at[j, 16 * g + i], arrived[part].at[j, here],
                        send.at[j], receive.at[j], part, step,
                    )
                    copy.start()
                    copies.append((copy, step))
        out_copies.append(copies)

    back_copies = []
    for j in range(2):
        for copy, step in out_copies[j]:
            wait_arrived(copy, step)
        loads = whole_copies([ref.at[j] for ref in arrived], buffers, load)
        for copy in loads:
            copy.start()
        for copy, step in out_copies[j]:
            wait_sent(copy, step)
        for copy in weights:
            copy.wait()
        for copy in loads:
            copy.wait()

        def expert_step(step, carry, j=j):
            expert_rows(step, buffers, x_ref)
            both = mul(x_ref[...], up_v[...])
            gate = both[:, :hidden_width]
            hidden = (gate / (1.0 + jnp.exp(-gate)) * both[:, hidden_width:]).astype(BF16)
            expert_results(step, mul(hidden, down_v[...]), [ref.at[j] for ref in stages])
            return carry

        lax.fori_loop(0, 4, expert_step, 0)
        if j == 0:
            weights = weight_copies(1)
            for copy in weights:
                copy.start()
        stores = whole_copies([ref.at[j] for ref in stages], [ref.at[j] for ref in staged], store)
        for copy in stores:
            copy.start()
        for copy in stores:
            copy.wait()
        copies = []
        for step in ORDER:
            for part in range(3):
                copy = plane_copy(
                    staged[part].at[j, plane_index(part, across(part, *step))],
                    returned[part].at[j, plane_index(part, (0, 0, 0, 0))],
                    send_back.at[j], receive_back.at[j], part, step,
                )
                copy.start()
                copies.append((copy, step))
        back_copies.append(copies)

    scatters = line_copies(lines, sums, scatter_semaphores, True)
    own, others = scatters[0:3], scatters[3:]
    row = lax.broadcasted_iota(jnp.int32, (2 * ROWS, TOK), 0).astype(F32)
    for j in range(2):
        for copy, step in back_copies[j]:
            wait_arrived(copy, step)
        loads = whole_copies([ref.at[j] for ref in returned], buffers, load)
        for copy in loads:
            copy.start()
        for n, d in enumerate((1, 3, 2, 0)):
            for part in range(3):
                if n == 0:
                    loads[part].wait()
                width = buffers[part].shape[2]
                a = lax.rem(line_place(part) + d, 4)
                tile = pl.ds(pl.multiple_of(a // 2 * 16, 16), 16)
                shift = (a % 2 * ROWS).astype(F32)
                mine = slice(32 * j, 32 * j + 32)
                slots = slot_ref[part, a, mine] + shift
                give = jnp.where(slots[:, None, :] == row, share_ref[part, a, mine][:, None, :], 0.0)
                high, low = halves(give.reshape(64 * ROWS, TOK))
                values = buffers[part][:, tile].reshape(64 * ROWS, width)
                both = mul(jnp.concatenate([high, low], axis=1), values, TN)
                if j == 0:
                    totals[part][a] = both[:TOK] + both[TOK:]
                else:
                    lines[part][a] = (totals[part][a] + both[:TOK] + both[TOK:]).astype(BF16)
                    copy = own[part] if d == 0 else others[3 * n + part]
                    copy.start()
    for part, (low, high) in enumerate(PARTS):
        for n in range(3):
            others[3 * n + part].wait()
        own[part].wait()
        total = mid_ref[:, low:high]
        for a in range(4):
            total = total + sums[part][a].astype(F32)
        out_ref[:, low:high] = total.astype(BF16)
    for copies in back_copies:
        for copy, step in copies:
            wait_sent(copy, step)


def moe(tables, mid, rows, up, down, top):
    dma = pltpu.SemaphoreType.DMA
    widths = [part.shape[1] for part in rows]
    exchange = [jax.ShapeDtypeStruct((2, 32, 4 * ROWS, width), BF16) for width in widths]
    return pl.pallas_call(
        functools.partial(moe_kernel, top),
        in_specs=[pl.BlockSpec(memory_space=pltpu.VMEM)] * 5 + [pl.BlockSpec(memory_space=pl.ANY)] * 2,
        out_specs=[pl.BlockSpec(memory_space=pltpu.VMEM)] + [pl.BlockSpec(memory_space=pl.ANY)] * 9,
        out_shape=[jax.ShapeDtypeStruct(mid.shape, BF16)] + exchange * 3,
        scratch_shapes=[pltpu.VMEM((4, TOK, width), BF16) for width in widths]
        + [pltpu.VMEM((2, 32, 4 * ROWS, width), BF16) for width in widths]
        + [pltpu.VMEM((32, 4 * ROWS, width), BF16) for width in widths]
        + [pltpu.VMEM((4, TOK, width), BF16) for width in widths]
        + [pltpu.VMEM((4, TOK, width), F32) for width in widths]
        + [pltpu.VMEM(up.shape[1:], BF16), pltpu.VMEM(down.shape[1:], BF16), pltpu.VMEM((256, up.shape[1]), BF16)]
        + [pltpu.VMEM((3, 4, 64, TOK), F32)] * 2
        + [dma((3, 4)), dma((3, 4)), dma((3,))] * 2
        + [dma((2, 3, 32))] * 4
        + [dma((3,)), dma((2,)), dma((3,))],
        compiler_params=pltpu.CompilerParams(
            collective_id=1, has_side_effects=True, vmem_limit_bytes=VMEM
        ),
        name="moe",
    )(tables, mid, *rows, up, down)[0]


def shards(
    query_rows,
    key_rows,
    value_rows,
    gate_z,
    log_decay,
    write_strength,
    norm_gain,
    out_weight,
    residual,
    post_gain,
    expert_ids,
    gate_scores,
    expert_up,
    expert_down,
):
    mid, rows_a, rows_b, rows_c, tables = mixer(
        query_rows[0], key_rows[0], value_rows[0], log_decay[0], write_strength[0], gate_z[0], norm_gain,
        residual[0], post_gain, jnp.transpose(expert_ids, (2, 0, 1)), jnp.transpose(gate_scores, (2, 0, 1)),
        out_weight, lax.axis_size("seq"),
    )
    rows = [rows_a, rows_b, rows_c]
    return moe(tables, mid, rows, expert_up, expert_down, expert_ids.shape[2])[None]


def solution(mesh):
    return jax.shard_map(
        shards,
        mesh=mesh,
        in_specs=(
            P("batch", "seq", None),
            P("batch", "seq", None),
            P("batch", "seq", None),
            P("batch", "seq", None),
            P("batch", None, "seq"),
            P("batch", None, "seq"),
            P(),
            P(),
            P("batch", "seq", None),
            P(),
            P("batch", "seq", None),
            P("batch", "seq", None),
            P(("seq", "batch"), None, None),
            P(("seq", "batch"), None, None),
        ),
        out_specs=P("batch", "seq", None),
        check_vma=False,
    )
```

```python
import functools

import jax
import jax.numpy as jnp
from jax import lax
from jax.experimental import pallas as pl
from jax.experimental.pallas import tpu as pltpu
from jax.sharding import PartitionSpec as P

TOK = 128
DK = 128
HV = 16
HK = 8
GROUPS = 2
ROWS = 8
MSG = 272
VMEM = 60 << 20
PARTS = ((0, 768), (768, 1408), (1408, 2048))
MESH = pl.DeviceIdType.MESH
EPSILON = 1e-06
PRECISE = lax.Precision.HIGHEST
F32 = jnp.float32
BF16 = jnp.bfloat16

NN = (((1,), (0,)), ((), ()))
NT = (((1,), (1,)), ((), ()))
TN = (((0,), (0,)), ((), ()))


def mul(a, b, dims=NN):
    return lax.dot_general(a, b, dims, preferred_element_type=F32)


def mul_precise(a, b, dims=NN):
    return lax.dot_general(a, b, dims, preferred_element_type=F32, precision=PRECISE)


def halves(a):
    high = a.astype(BF16)
    return high, (a - high.astype(F32)).astype(BF16)


def axis_names():
    seq = lax.axis_index("seq")
    return (lax.div(seq, 8), lax.rem(lax.div(seq, 2), 4), lax.rem(seq, 2), lax.axis_index("batch"))


def device_at(offset):
    z, x, core, y = axis_names()
    dz, dx, dcore, dy = offset
    seq = lax.rem(z + dz, 4) * 8 + lax.rem(x + dx, 4) * 2 + lax.rem(core + dcore, 2)
    return (seq, lax.rem(y + dy, 4))


def greet(offsets):
    barrier = pltpu.get_barrier_semaphore()
    for offset in offsets:
        pl.semaphore_signal(barrier, inc=1, device_id=device_at(offset), device_id_type=MESH)
    pl.semaphore_wait(barrier, len(offsets))


def along(part, d):
    return ((0, 0, 0, d), (0, d, 0, 0), (d, 0, 0, 0))[part]


def across(part, p, q, dcore):
    return ((p, q, dcore, 0), (p, 0, dcore, q), (0, p, dcore, q))[part]


def line_place(part):
    z, x, _, y = axis_names()
    return (y, x, z)[part]


def plane_index(part, offset):
    z, x, core, y = axis_names()
    dz, dx, dcore, dy = offset
    z, x, y = lax.rem(z + dz, 4), lax.rem(x + dx, 4), lax.rem(y + dy, 4)
    first, second = ((z, x), (z, y), (x, y))[part]
    return (first * 4 + second) * 2 + lax.rem(core + dcore, 2)


PAIRS = (
    ((1, 1), (3, 3), (1, 3), (3, 1)),
    ((2, 2),),
    ((1, 0), (3, 0), (0, 1), (0, 3)),
    ((2, 0), (0, 2)),
    ((2, 1), (2, 3)),
    ((1, 2), (3, 2)),
)


def line_copies(sources, targets, semaphores, scatter):
    send, receive, own = semaphores
    copies = []
    for part in range(3):
        place = line_place(part)
        source = sources[part].at[place] if scatter else sources[part]
        copies.append(pltpu.make_async_copy(source, targets[part].at[place], own.at[part]))
    for d in (1, 3, 2):
        for part in range(3):
            place = line_place(part)
            source = sources[part].at[lax.rem(place + d, 4)] if scatter else sources[part]
            copies.append(pltpu.make_async_remote_copy(
                source, targets[part].at[place], send.at[part, d], receive.at[part, d],
                device_id=device_at(along(part, d)), device_id_type=MESH,
            ))
    return copies


def local_terms(g, q_ref, k_ref, v_ref, ld_ref, bt_ref, map_ref, reader_ref, local_ref, n_ref, x_ref, s_ref):
    heads = HV // GROUPS
    row = lax.broadcasted_iota(jnp.int32, (TOK, TOK), 0)
    col = lax.broadcasted_iota(jnp.int32, (TOK, TOK), 1)
    ld = ld_ref[g]
    cum_row = mul_precise(ld, (row <= col).astype(F32))
    cum_col = mul_precise((row >= col).astype(F32), ld, NT)
    beta_col = bt_ref[g].T
    units = []
    for pair in range(heads // 2):
        key_head = g * (heads // 2) + pair
        lanes = slice(key_head * DK, (key_head + 1) * DK)
        k_raw = k_ref[:, lanes]
        q_raw = q_ref[:, lanes]
        k_full = k_raw.astype(F32)
        q_full = q_raw.astype(F32)
        k_scale = lax.rsqrt(jnp.sum(k_full * k_full, axis=-1, keepdims=True) + EPSILON)
        q_scale = lax.rsqrt(jnp.sum(q_full * q_full, axis=-1, keepdims=True) + EPSILON) * DK ** (-0.5)
        k_unit = k_full * k_scale
        k_high, k_low = halves(k_unit)
        right = jnp.concatenate([k_high, k_low], axis=1)
        key_key = mul(jnp.concatenate([k_raw, k_raw], axis=1), right, NT) * k_scale
        query_key = mul(jnp.concatenate([q_raw, q_raw], axis=1), right, NT) * q_scale
        units.append((k_unit, q_full * q_scale))
        for h in (2 * pair, 2 * pair + 1):
            gap = cum_col[:, h:h + 1] - cum_row[h:h + 1, :]
            decay = jnp.where(row >= col, jnp.exp(jnp.minimum(gap, 0.0)), 0.0)
            s_ref[h] = (decay * query_key).astype(BF16)
            system = jnp.where(row > col, decay * key_key, 0.0) * beta_col[:, h:h + 1]
            n_ref[h] = system
            x_ref[h] = jnp.where((row ^ col) == 1, -system, 0.0)
    for level in range(1, 7):
        cross = ((row >> level) ^ (col >> level)) == 1
        left = []
        for h in range(heads):
            part = jnp.where(cross, n_ref[h], 0.0)
            left.append(part + mul(x_ref[h].astype(BF16), part.astype(BF16)))
        for h in range(heads):
            old = x_ref[h]
            x_ref[h] = old - left[h] - mul(left[h].astype(BF16), old.astype(BF16))
    line = lax.broadcasted_iota(jnp.int32, (16, DK), 0)
    for h in range(heads):
        k_unit, q_unit = units[h // 2]
        cum = cum_col[:, h:h + 1]
        last = cum_row[h:h + 1, TOK - 1:TOK]
        beta = beta_col[:, h:h + 1]
        gamma = jnp.exp(cum)
        head = g * heads + h
        value = v_ref[:, head * DK:(head + 1) * DK].astype(F32) * beta
        right = jnp.concatenate([value, k_unit * (beta * gamma)], axis=1)
        write = (right + mul(x_ref[h].astype(BF16), right.astype(BF16))).astype(BF16)
        tail = (jnp.exp(last - cum) * k_unit).astype(BF16)
        moved = mul(write, tail, TN)
        read = mul(s_ref[h], write)
        local_ref[head] = read[:, :DK]
        reader_ref[head] = (gamma * q_unit - read[:, DK:]).astype(BF16)
        whole = jnp.exp(jnp.broadcast_to(last, (16, DK)))
        part0 = whole.astype(BF16)
        part1 = (whole - part0.astype(F32)).astype(BF16)
        part2 = (whole - part0.astype(F32) - part1.astype(F32)).astype(BF16)
        parts = jnp.where(line == 0, part0.astype(F32), jnp.where(line == 1, part1.astype(F32), part2.astype(F32)))
        map_ref[head, 0:128] = (-moved[DK:]).astype(BF16)
        map_ref[head, 128:256] = moved[:DK].astype(BF16)
        map_ref[head, 256:272] = jnp.where(line < 3, parts, 0.0).astype(BF16)


def mixer_kernel(
    q_ref, k_ref, v_ref, ld_ref, bt_ref, gate_ref, gain_ref, resid_ref, post_ref, ids_hbm, scores_hbm, weight_ref,
    mid_ref, a_ref, b_ref, c_ref, tables_ref,
    map_ref, reader_ref, local_ref, n_ref, x_ref, s_ref, weight_v, normed_ref, state_ref, inbox, outbox, table_ref, ids_ref, scores_ref,
    send, receive, send_back, receive_back, fetch, *lines,
):
    seq, batch = lax.axis_index("seq"), lax.axis_index("batch")
    z, x, core = seq // 8, seq // 2 % 4, seq % 2
    count = inbox.shape[0]
    heads = HV // GROUPS
    owned = (z + x) % 2 * heads + z * 2 + x // 2

    weights = pltpu.make_async_copy(weight_ref, weight_v, fetch.at[0])
    routing = (
        pltpu.make_async_copy(ids_hbm, ids_ref, fetch.at[1]),
        pltpu.make_async_copy(scores_hbm, scores_ref, fetch.at[2]),
    )
    for copy in routing:
        copy.start()
    weights.start()
    barrier = pltpu.get_barrier_semaphore()
    for other in range(1, count):
        pl.semaphore_signal(
            barrier, inc=1, device_id=(lax.rem(seq + other, count), batch), device_id_type=MESH
        )
    for d in (1, 2, 3):
        pl.semaphore_signal(barrier, inc=1, device_id=device_at((0, 0, 0, d)), device_id_type=MESH)

    def to_owner(g, n):
        i = lax.rem(n + z * 4 + x, heads)
        head = g * heads + i
        to_z = i // 2
        owner = (to_z * 4 + i % 2 * 2 + (to_z + g) % 2) * 2
        remote = pltpu.make_async_remote_copy(
            map_ref.at[head], inbox.at[seq], send.at[head], receive.at[seq],
            device_id=(owner, batch), device_id_type=MESH,
        )
        own = pltpu.make_async_copy(map_ref.at[head], inbox.at[seq], receive.at[seq])
        return owner, remote, own

    def ship(g):
        for n in range(heads):
            owner, remote, own = to_owner(g, n)

            @pl.when(owner == seq)
            def _():
                own.start()

            @pl.when(owner != seq)
            def _():
                remote.start()

    local_args = (q_ref, k_ref, v_ref, ld_ref, bt_ref, map_ref, reader_ref, local_ref, n_ref, x_ref, s_ref)
    local_terms(0, *local_args)
    pl.semaphore_wait(barrier, count + 2)
    ship(0)
    for copy in routing:
        copy.wait()
    top = ids_ref.shape[0]
    numbers = jnp.concatenate([ids_ref[k] for k in range(top)], axis=0).astype(F32)
    scores = jnp.concatenate([scores_ref[k] for k in range(top)], axis=0)
    high, low = halves(scores / jnp.sum(scores, axis=0, keepdims=True))
    spare = jnp.zeros((16 - numbers.shape[0], TOK), F32)
    for n, value in enumerate((numbers, high.astype(F32), low.astype(F32))):
        table_ref[16 * n:16 * n + 16] = jnp.concatenate([value, spare], axis=0).astype(BF16)
    tables = line_copies((table_ref,) * 3, [tables_ref.at[part] for part in range(3)], lines, False)
    for copy in tables:
        copy.start()
    local_terms(1, *local_args)
    ship(1)

    def back(place):
        return pltpu.make_async_remote_copy(
            outbox.at[place], state_ref.at[owned], send_back.at[place], receive_back.at[owned],
            device_id=(place, batch), device_id_type=MESH,
        )

    @pl.when(core == 0)
    def _():
        def step(place, state):
            high, low = halves(state)
            outbox[place] = high

            @pl.when(place == seq)
            def _():
                pltpu.make_async_copy(outbox.at[seq], state_ref.at[owned], receive_back.at[owned]).start()

            @pl.when(place != seq)
            def _():
                back(place).start()

            both = mul(jnp.concatenate([high, low], axis=0), inbox[place, 0:128])
            parts = inbox[place, 256:272].astype(F32)
            gamma = parts[0:1] + parts[1:2] + parts[2:3]
            return state * gamma + (both[:DK] + both[DK:]) + inbox[place, 128:256].astype(F32)

        def steps(group, state):
            for n in range(4):
                place = group * 4 + n
                pltpu.make_async_copy(inbox.at[place], inbox.at[place], receive.at[place]).wait()
            for n in range(4):
                state = step(group * 4 + n, state)
            return state

        lax.fori_loop(0, count // 4, steps, jnp.zeros((DK, DK), F32))

    for h in range(HV):
        pltpu.make_async_copy(state_ref.at[h], state_ref.at[h], receive_back.at[h]).wait()
        kept = mul(reader_ref[h], state_ref[h], NT) + local_ref[h]
        scaled = kept * lax.rsqrt(jnp.mean(kept * kept, axis=-1, keepdims=True) + EPSILON)
        gate = gate_ref[:, h * DK:(h + 1) * DK].astype(F32)
        normed_ref[:, h * DK:(h + 1) * DK] = (
            scaled * gain_ref[...] * (gate / (1.0 + jnp.exp(-gate)))
        ).astype(BF16)
    weights.wait()
    width = mid_ref.shape[1]
    tile = 512
    total = jnp.zeros((TOK, 1), F32)
    for start in range(0, width, tile):
        lanes = slice(start, start + tile)
        mid = resid_ref[:, lanes].astype(F32) + mul(normed_ref[...], weight_v[:, lanes])
        mid_ref[:, lanes] = mid
        total = total + jnp.sum(mid * mid, axis=-1, keepdims=True)
    scale = lax.rsqrt(total / width + EPSILON)
    for ref, (low, high) in zip((a_ref, b_ref, c_ref), PARTS):
        ref[...] = (mid_ref[:, low:high] * scale * post_ref[:, low:high]).astype(BF16)

    for g in range(GROUPS):
        for n in range(heads):
            owner, remote, _ = to_owner(g, n)

            @pl.when(owner != seq)
            def _():
                remote.wait_send()

    @pl.when(core == 0)
    def _():
        def sent(place, carry):
            @pl.when(place != seq)
            def _():
                back(place).wait_send()

            return carry

        lax.fori_loop(0, count, sent, 0)

    for copy in tables:
        copy.wait()


def mixer(query, key, value, log_decay, strength, gate, gain, resid, post, ids, scores, weight, count):
    heads = HV // GROUPS
    width = weight.shape[1]
    dma = pltpu.SemaphoreType.DMA
    vmem = pltpu.VMEM
    return pl.pallas_call(
        mixer_kernel,
        in_specs=[pl.BlockSpec(memory_space=vmem)] * 9 + [pl.BlockSpec(memory_space=pl.ANY)] * 3,
        out_specs=[pl.BlockSpec(memory_space=vmem)] * 5,
        out_shape=[jax.ShapeDtypeStruct((TOK, width), F32)]
        + [jax.ShapeDtypeStruct((TOK, high - low), BF16) for low, high in PARTS]
        + [jax.ShapeDtypeStruct((3, 4, 48, TOK), BF16)],
        scratch_shapes=[
            vmem((HV, MSG, DK), BF16),
            vmem((HV, TOK, DK), BF16),
            vmem((HV, TOK, DK), F32),
            vmem((heads, TOK, TOK), F32),
            vmem((heads, TOK, TOK), F32),
            vmem((heads, TOK, TOK), BF16),
            vmem(weight.shape, BF16),
            vmem((TOK, weight.shape[0]), BF16),
            vmem((HV, DK, DK), BF16),
            vmem((count, MSG, DK), BF16),
            vmem((count, DK, DK), BF16),
            vmem((48, TOK), BF16),
            vmem(ids.shape, jnp.int32),
            vmem(scores.shape, F32),
            dma((HV,)),
            dma((count,)),
            dma((count,)),
            dma((HV,)),
            dma((3,)),
            dma((3, 4)),
            dma((3, 4)),
            dma((3,)),
        ],
        compiler_params=pltpu.CompilerParams(
            collective_id=0, has_side_effects=True, vmem_limit_bytes=VMEM
        ),
        name="mixer",
    )(
        query, key, value, log_decay.reshape(GROUPS, heads, TOK), strength.reshape(GROUPS, heads, TOK),
        gate, gain[None], resid, post[None], ids, scores, weight,
    )


ORDER = [(p, q, dcore) for group in PAIRS for dcore in (0, 1) for p, q in group] + [(0, 0, 1), (0, 0, 0)]


def plane_copy(source, target, send, receive, part, step):
    p, q, dcore = step
    offset = across(part, p, q, dcore)
    slot = p * 8 + q * 2 + dcore
    if step == (0, 0, 0):
        return pltpu.make_async_copy(source, target, receive.at[part, slot])
    return pltpu.make_async_remote_copy(
        source, target, send.at[part, slot], receive.at[part, slot],
        device_id=device_at(offset), device_id_type=MESH,
    )


def wait_sent(copy, step):
    if step != (0, 0, 0):
        copy.wait_send()


def wait_arrived(copy, step):
    if step == (0, 0, 0):
        copy.wait()
    else:
        copy.wait_recv()


def plane_offsets():
    return sorted(set(across(part, *step) for part in range(3) for step in ORDER) - {(0, 0, 0, 0)})


def picked(slot):
    rows = lax.broadcasted_iota(jnp.int32, (ROWS, TOK), 0).astype(F32)
    return slot[..., None, :] == rows


def whole_copies(sources, targets, semaphores):
    return [pltpu.make_async_copy(sources[part], targets[part], semaphores.at[part]) for part in range(3)]


def expert_rows(step, buffers, x_ref):
    a_ref, b_ref, c_ref = buffers
    wa, wb = a_ref.shape[2], b_ref.shape[2]
    pair, core = step // 2, step % 2
    tile = pl.ds(pl.multiple_of(pair * 16, 16), 16)
    parts_c = [[c_ref[(x * 4 + y) * 2 + core, tile].astype(F32) for y in range(4)] for x in range(4)]
    for n in range(2):
        z = pair * 2 + n
        parts_b = [b_ref[(z * 4 + y) * 2 + core].astype(F32) for y in range(4)]
        for x in range(4):
            rows = slice((n * 4 + x) * 32, (n * 4 + x) * 32 + 32)
            x_ref[rows, 0:wa] = a_ref[(z * 4 + x) * 2 + core]
            x_ref[rows, wa:wa + wb] = jnp.concatenate(
                [parts_b[y][x * ROWS:(x + 1) * ROWS] for y in range(4)], axis=0
            ).astype(BF16)
            x_ref[rows, wa + wb:] = jnp.concatenate(
                [parts_c[x][y][n * ROWS:(n + 1) * ROWS] for y in range(4)], axis=0
            ).astype(BF16)


def expert_results(step, result, stages):
    a_ref, b_ref, c_ref = stages
    wa, wb = a_ref.shape[2], b_ref.shape[2]
    pair, core = step // 2, step % 2
    tile = pl.ds(pl.multiple_of(pair * 16, 16), 16)

    def piece(n, x, y, low, high):
        start = ((n * 4 + x) * 4 + y) * ROWS
        return result[start:start + ROWS, low:high]

    for n in range(2):
        z = pair * 2 + n
        for x in range(4):
            start = (n * 4 + x) * 32
            a_ref[(z * 4 + x) * 2 + core] = result[start:start + 32, 0:wa].astype(BF16)
        for y in range(4):
            b_ref[(z * 4 + y) * 2 + core] = jnp.concatenate(
                [piece(n, x, y, wa, wa + wb) for x in range(4)], axis=0
            ).astype(BF16)
    for x in range(4):
        for y in range(4):
            c_ref[(x * 4 + y) * 2 + core, tile] = jnp.concatenate(
                [piece(n, x, y, wa + wb, result.shape[1]) for n in range(2)], axis=0
            ).astype(BF16)


def fill_slots(tables_ref, slot_ref, share_ref, top):
    z, x, _, y = axis_names()
    line = lax.broadcasted_iota(jnp.int32, (64, TOK), 0)
    half, place = line // 32, line % 32
    first, second, side = place // 8, place // 2 % 4, place % 2
    device = (
        place * 4 + y,
        (first * 8 + x * 2 + side) * 4 + second,
        (z * 8 + first * 2 + side) * 4 + second,
    )
    row = lax.broadcasted_iota(jnp.int32, (TOK, TOK), 0)
    col = lax.broadcasted_iota(jnp.int32, (TOK, TOK), 1)
    earlier = (row < col).astype(F32).astype(BF16)
    for part in range(3):
        expert = (device[part] * 2 + half).astype(F32)
        for a in range(4):
            table = tables_ref[part, a].astype(F32)
            chosen = jnp.zeros((64, TOK), F32)
            given = jnp.zeros((64, TOK), F32)
            for k in range(top):
                named = table[k:k + 1] == expert
                share = table[16 + k:17 + k] + table[32 + k:33 + k]
                chosen = jnp.where(named, 1.0, chosen)
                given = jnp.where(named, share, given)
            rank = mul(chosen.astype(BF16), earlier)
            slot_ref[part, a] = jnp.where(chosen > 0, rank, -1.0)
            share_ref[part, a] = given


def moe_kernel(top, *refs):
    tables_ref, mid_ref, rows, up_ref, down_ref = refs[0], refs[1], refs[2:5], refs[5], refs[6]
    out_ref, arrived, returned, staged = refs[7], refs[8:11], refs[11:14], refs[14:17]
    lines, stages, buffers, sums, totals = refs[17:20], refs[20:23], refs[23:26], refs[26:29], refs[29:32]
    up_v, down_v, x_ref, slot_ref, share_ref, take_ref = refs[32:38]
    gather_semaphores, scatter_semaphores = refs[38:41], refs[41:44]
    send, receive, send_back, receive_back, load, fetch, store = refs[44:51]
    hidden_width = down_ref.shape[1]

    def weight_copies(j):
        return (
            pltpu.make_async_copy(up_ref.at[j], up_v, fetch.at[0]),
            pltpu.make_async_copy(down_ref.at[j], down_v, fetch.at[1]),
        )

    weights = weight_copies(0)
    for copy in weights:
        copy.start()
    greet(plane_offsets())
    gathers = line_copies(rows, lines, gather_semaphores, False)
    for copy in gathers:
        copy.start()
    fill_slots(tables_ref, slot_ref, share_ref, top)
    for j in range(2):
        for g in range(2):
            for part in range(3):
                places = [plane_index(part, across(part, *step)) for step in ORDER[16 * g:16 * g + 16]]

                def ready(a, carry, part=part, places=places, g=g, j=j):
                    slots = jnp.concatenate(
                        [slot_ref[part, a, pl.ds(place + 32 * j, 1)] for place in places], axis=0
                    )
                    take = jnp.where(picked(slots), 1.0, 0.0).reshape(16 * ROWS, TOK).astype(BF16)
                    take_ref[(part * 2 + j) * 2 + g, a] = take
                    return carry

                lax.fori_loop(0, 4, ready, 0)
    for copy in gathers:
        copy.wait()

    out_copies = []
    for j in range(2):
        copies = []
        for g in range(2):
            steps = ORDER[16 * g:16 * g + 16]
            group = slice(16 * g, 16 * g + 16)
            stores = []
            for part in range(3):

                def fill(pair, carry, part=part, group=group, g=g, j=j):
                    packed = []
                    for n in range(2):
                        a = pair * 2 + n
                        take = take_ref[(part * 2 + j) * 2 + g, a]
                        packed.append(mul(take, lines[part][a]).reshape(16, ROWS, lines[part].shape[2]))
                    tile = pl.ds(pl.multiple_of(pair * 16, 16), 16)
                    stages[part][j, group, tile] = jnp.concatenate(packed, axis=1).astype(BF16)
                    return carry

                lax.fori_loop(0, 2, fill, 0)
                stores.append(pltpu.make_async_copy(
                    stages[part].at[j, group], staged[part].at[j, group], store.at[part]
                ))
                stores[part].start()
            for copy in stores:
                copy.wait()
            for i, step in enumerate(steps):
                for part in range(3):
                    here = plane_index(part, (0, 0, 0, 0))
                    copy = plane_copy(
                        staged[part].at[j, 16 * g + i], arrived[part].at[j, here],
                        send.at[j], receive.at[j], part, step,
                    )
                    copy.start()
                    copies.append((copy, step))
        out_copies.append(copies)

    back_copies = []
    for j in range(2):
        for copy, step in out_copies[j]:
            wait_arrived(copy, step)
        loads = whole_copies([ref.at[j] for ref in arrived], buffers, load)
        for copy in loads:
            copy.start()
        for copy, step in out_copies[j]:
            wait_sent(copy, step)
        for copy in weights:
            copy.wait()
        for copy in loads:
            copy.wait()

        def expert_step(step, carry, j=j):
            expert_rows(step, buffers, x_ref)
            both = mul(x_ref[...], up_v[...])
            gate = both[:, :hidden_width]
            hidden = (gate / (1.0 + jnp.exp(-gate)) * both[:, hidden_width:]).astype(BF16)
            expert_results(step, mul(hidden, down_v[...]), [ref.at[j] for ref in stages])
            return carry

        lax.fori_loop(0, 4, expert_step, 0)
        if j == 0:
            weights = weight_copies(1)
            for copy in weights:
                copy.start()
        stores = whole_copies([ref.at[j] for ref in stages], [ref.at[j] for ref in staged], store)
        for copy in stores:
            copy.start()
        for copy in stores:
            copy.wait()
        copies = []
        for step in ORDER:
            for part in range(3):
                copy = plane_copy(
                    staged[part].at[j, plane_index(part, across(part, *step))],
                    returned[part].at[j, plane_index(part, (0, 0, 0, 0))],
                    send_back.at[j], receive_back.at[j], part, step,
                )
                copy.start()
                copies.append((copy, step))
        back_copies.append(copies)

    scatters = line_copies(lines, sums, scatter_semaphores, True)
    own, others = scatters[0:3], scatters[3:]
    row = lax.broadcasted_iota(jnp.int32, (2 * ROWS, TOK), 0).astype(F32)
    for j in range(2):
        for copy, step in back_copies[j]:
            wait_arrived(copy, step)
        loads = whole_copies([ref.at[j] for ref in returned], buffers, load)
        for copy in loads:
            copy.start()
        for d in (2, 1, 3, 0):
            for part in range(3):
                if d == 2:
                    loads[part].wait()
                width = buffers[part].shape[2]
                a = lax.rem(line_place(part) + d, 4)
                tile = pl.ds(pl.multiple_of(a // 2 * 16, 16), 16)
                shift = (a % 2 * ROWS).astype(F32)
                mine = slice(32 * j, 32 * j + 32)
                slots = slot_ref[part, a, mine] + shift
                give = jnp.where(slots[:, None, :] == row, share_ref[part, a, mine][:, None, :], 0.0)
                high, low = halves(give.reshape(64 * ROWS, TOK))
                values = buffers[part][:, tile].reshape(64 * ROWS, width)
                both = mul(jnp.concatenate([high, low], axis=1), values, TN)
                if j == 0:
                    totals[part][a] = both[:TOK] + both[TOK:]
                else:
                    lines[part][a] = (totals[part][a] + both[:TOK] + both[TOK:]).astype(BF16)
                    copy = own[part] if d == 0 else others[3 * (0, 0, 2, 1)[d] + part]
                    copy.start()
    for part, (low, high) in enumerate(PARTS):
        for n in range(3):
            others[3 * n + part].wait()
        own[part].wait()
        total = mid_ref[:, low:high]
        for a in range(4):
            total = total + sums[part][a].astype(F32)
        out_ref[:, low:high] = total.astype(BF16)
    for copies in back_copies:
        for copy, step in copies:
            wait_sent(copy, step)


def moe(tables, mid, rows, up, down, top):
    dma = pltpu.SemaphoreType.DMA
    widths = [part.shape[1] for part in rows]
    exchange = [jax.ShapeDtypeStruct((2, 32, 4 * ROWS, width), BF16) for width in widths]
    return pl.pallas_call(
        functools.partial(moe_kernel, top),
        in_specs=[pl.BlockSpec(memory_space=pltpu.VMEM)] * 5 + [pl.BlockSpec(memory_space=pl.ANY)] * 2,
        out_specs=[pl.BlockSpec(memory_space=pltpu.VMEM)] + [pl.BlockSpec(memory_space=pl.ANY)] * 9,
        out_shape=[jax.ShapeDtypeStruct(mid.shape, BF16)] + exchange * 3,
        scratch_shapes=[pltpu.VMEM((4, TOK, width), BF16) for width in widths]
        + [pltpu.VMEM((2, 32, 4 * ROWS, width), BF16) for width in widths]
        + [pltpu.VMEM((32, 4 * ROWS, width), BF16) for width in widths]
        + [pltpu.VMEM((4, TOK, width), BF16) for width in widths]
        + [pltpu.VMEM((4, TOK, width), F32) for width in widths]
        + [pltpu.VMEM(up.shape[1:], BF16), pltpu.VMEM(down.shape[1:], BF16), pltpu.VMEM((256, up.shape[1]), BF16)]
        + [pltpu.VMEM((3, 4, 64, TOK), F32)] * 2 + [pltpu.VMEM((12, 4, 16 * ROWS, TOK), BF16)]
        + [dma((3, 4)), dma((3, 4)), dma((3,))] * 2
        + [dma((2, 3, 32))] * 4
        + [dma((3,)), dma((2,)), dma((3,))],
        compiler_params=pltpu.CompilerParams(
            collective_id=1, has_side_effects=True, vmem_limit_bytes=VMEM
        ),
        name="moe",
    )(tables, mid, *rows, up, down)[0]


def shards(
    query_rows,
    key_rows,
    value_rows,
    gate_z,
    log_decay,
    write_strength,
    norm_gain,
    out_weight,
    residual,
    post_gain,
    expert_ids,
    gate_scores,
    expert_up,
    expert_down,
):
    mid, rows_a, rows_b, rows_c, tables = mixer(
        query_rows[0], key_rows[0], value_rows[0], log_decay[0], write_strength[0], gate_z[0], norm_gain,
        residual[0], post_gain, jnp.transpose(expert_ids, (2, 0, 1)), jnp.transpose(gate_scores, (2, 0, 1)),
        out_weight, lax.axis_size("seq"),
    )
    rows = [rows_a, rows_b, rows_c]
    return moe(tables, mid, rows, expert_up, expert_down, expert_ids.shape[2])[None]


def solution(mesh):
    return jax.shard_map(
        shards,
        mesh=mesh,
        in_specs=(
            P("batch", "seq", None),
            P("batch", "seq", None),
            P("batch", "seq", None),
            P("batch", "seq", None),
            P("batch", None, "seq"),
            P("batch", None, "seq"),
            P(),
            P(),
            P("batch", "seq", None),
            P(),
            P("batch", "seq", None),
            P("batch", "seq", None),
            P(("seq", "batch"), None, None),
            P(("seq", "batch"), None, None),
        ),
        out_specs=P("batch", "seq", None),
        check_vma=False,
    )
```
